256 devices in a mesh: replica: 8 (over y, z_hi), fsdp: 32 (over z_lo, x, core).
Axes of the slice: x: 4, y: 4, z: 8 (z_hi: 2, z_lo: 4; z = z_hi * 4 + z_lo), core: 2. Of those that a mesh axis runs over, the one named last changes fastest.
Arguments:
- residual: bfloat16 [8, 8192, 4608], P('replica', 'fsdp'), may hold values from -6 to 6
- cotangent: bfloat16 [8, 8192, 1024], P('replica', 'fsdp'), may hold values from -6 to 6
- norm_gain: float32 [8, 4608], P('replica'), may hold values from -0.5 to 0.5
- master: float32 [8, 4608, 1024], P('replica', 'fsdp'), may hold values from -6 to 6
- first_moment: float32 [8, 4608, 1024], P('replica', 'fsdp'), may hold values from -6 to 6
- second_moment: float32 [8, 4608, 1024], P('replica', 'fsdp'), may hold values from 0.05 to 2
- anchor: float32 [4608, 1024], P('fsdp'), may hold values from -6 to 6
- outer_momentum: float32 [4608, 1024], P('fsdp'), may hold values from -4 to 4
- history: float32 [8, 4, 768, 1024], P('replica', None, 'fsdp'), may hold values from -6 to 6
- fragment: int32 [576], replicated, may hold values from 0 to 5, as said below
- delay: int32 [8, 96], P('replica', 'fsdp'), may hold values from 1 to 4
Outputs:
- values: bfloat16 [8, 8192, 1024], P('replica', 'fsdp')
- input_grad: bfloat16 [8, 8192, 4608], P('replica', 'fsdp')
- gain_grad: float32 [8, 4608], P('replica')
- new_master: float32 [8, 4608, 1024], P('replica', 'fsdp')
- new_first: float32 [8, 4608, 1024], P('replica', 'fsdp')
- new_second: float32 [8, 4608, 1024], P('replica', 'fsdp')
- new_anchor: float32 [4608, 1024], P('fsdp')
- new_momentum: float32 [4608, 1024], P('fsdp')
The draws below stay inside these ranges and needn't reach their ends.
Inputs may be any that keep to these rules, and one draw needn't show every extreme that they name: Each aligned run of 6 row blocks (blocks 0 to 5, 6 to 11 and so on) holds every fragment number exactly once.
All inputs are finite; a program needn't handle non-finite values.
Results may differ from the reference program's by a relative error of at most 0.013.
Values may be sent and summed in bfloat16 or wider, within the bound.
A program may use at most 128 MiB of HBM per device.

```python
import math
import jax
import jax.numpy as jnp
from jax import lax

D = 4608
DV = 1024
TOKENS = 8192
FRAGS = 6
FR_ROWS = 8
HIST = 4
N_REPLICA = 8


def draw_fragment(key, part):
    key = jax.random.fold_in(key, 11)
    groups = D // (FR_ROWS * FRAGS)
    scores = jax.random.randint(key, (groups, FRAGS), 0, 1000000, dtype=jnp.int32)
    distinct = scores * FRAGS + jnp.arange(FRAGS, dtype=jnp.int32)[None, :]
    order = jnp.argsort(distinct, axis=1).astype(jnp.int32)
    return order.reshape(groups * FRAGS)


def set_ends(values, rng, smallest, high):
    longest = values.shape.index(max(values.shape))
    spots = []
    for shift in (0, 1):
        where = [jax.random.randint(jax.random.fold_in(rng, axis), (), 0, length) for axis, length in enumerate(values.shape)]
        where[longest] = (where[longest] + shift) % values.shape[longest]
        spots.append(tuple(where))
    return values.at[spots[0]].set(smallest).at[spots[1]].set(high)


def strengthened(entries, rng, source, target, parts, factor):
    owner, partner = [(jnp.arange(entries.shape[position]) // (entries.shape[position] // parts)).reshape([-1 if axis == position else 1 for axis in range(entries.ndim)]) for position in (source, target)]
    chosen = jax.random.permutation(rng, parts)[partner]
    strong = (owner == chosen) | (owner == (partner + parts // 2) % parts)
    return jnp.where(strong, factor * entries, entries)


def level_of(rng, dims, pieces, low, top_value):
    factor_of = 1.0
    for dim, blocks in pieces:
        heights = jax.random.uniform(jax.random.fold_in(jax.random.fold_in(rng, 6), dim), (blocks,), jnp.float32, low / len(pieces), top_value / len(pieces))
        factor_of = factor_of * jnp.repeat(jnp.exp(heights), dims[dim] // blocks).reshape((-1,) + (1,) * (len(dims) - 1 - dim))
    return factor_of


def centred(rng, dims, deviation, limit, shards=(), kind=jnp.bfloat16):
    entries = deviation * jax.random.normal(rng, dims, jnp.float32)
    if shards:
        entries = entries * level_of(rng, dims, shards, -0.22, 0.18)
    return jnp.clip(entries, -limit, limit).astype(kind)


def heavy_noise(rng, dims, width, most, shards, heavy, kind=jnp.bfloat16):
    result = width * jax.random.normal(rng, dims, jnp.float32)
    if shards:
        result = result * level_of(rng, dims, shards, -0.22, 0.18)
    return jnp.clip(strengthened(result, jax.random.fold_in(rng, 3), *heavy), -most, most).astype(kind)


def setup_inputs(seed: int = 0) -> dict:
    keys = jax.random.split(jax.random.key(seed), 12)
    residual = heavy_noise(keys[0], (N_REPLICA, TOKENS, D), 1.0, 6.0, ((0, 8), (1, 32)), (1, 2, 32, 2.75))
    cotangent = centred(keys[1], (N_REPLICA, TOKENS, DV), 1.0, 6.0, ((0, 8), (1, 32)))
    norm_gain = jnp.clip(jax.random.uniform(keys[2], (N_REPLICA, D), jnp.float32, -0.5, 0.5) * level_of(keys[2], (N_REPLICA, D), ((0, 8),), -0.4, 0.0), -0.5, 0.5)
    master = centred(keys[3], (N_REPLICA, D, DV), 1.0, 6.0, ((0, 8), (1, 32)), jnp.float32)
    first_moment = centred(keys[4], (N_REPLICA, D, DV), 1.0, 6.0, ((0, 8), (1, 32)), jnp.float32)
    second_moment = jnp.clip(jnp.exp(math.log(2.0) - 3.6888794 * jax.random.uniform(keys[5], (N_REPLICA, D, DV), jnp.float32) ** level_of(keys[5], (N_REPLICA, D, DV), ((0, 8), (1, 32)), -0.2, 0.2)), 0.05, 2.0)
    anchor = centred(keys[6], (D, DV), 1.0, 6.0, ((0, 32),), jnp.float32)
    outer_momentum = centred(keys[7], (D, DV), 0.5, 4.0, ((0, 32),), jnp.float32)
    history = centred(keys[8], (N_REPLICA, HIST, D // FRAGS, DV), 1.0, 6.0, ((0, 8), (2, 32)), jnp.float32)
    fragment = draw_fragment(jax.random.fold_in(keys[11], 71), 0)
    delay = set_ends(jax.random.randint(keys[10], (N_REPLICA, D // (FRAGS * FR_ROWS)), 1, HIST + 1), jax.random.fold_in(keys[10], 1), 1, HIST).astype(jnp.int32)
    return dict(residual=residual, cotangent=cotangent, norm_gain=norm_gain, master=master, first_moment=first_moment, second_moment=second_moment, anchor=anchor, outer_momentum=outer_momentum, history=history, fragment=fragment, delay=delay)


norm_eps = 1e-06
beta_one = 0.9
beta_two = 0.95
inner_rate = 0.01
weight_decay = 0.1
adam_eps = 1e-08
outer_beta = 0.9
outer_rate = 0.7
mix_weight = 0.5

def block_index(table):
    count = table.shape[0] // FRAGS
    order = jnp.argsort(jnp.where(table == 0, 0, 1).astype(jnp.int32), stable=True)
    return order[:count].astype(jnp.int32)

def take_part(array, chosen):
    view = array.reshape(array.shape[0] // FR_ROWS, FR_ROWS, array.shape[1])
    return view[chosen].reshape(chosen.shape[0] * FR_ROWS, array.shape[1])

def put_part(array, part, chosen):
    view = array.reshape(array.shape[0] // FR_ROWS, FR_ROWS, array.shape[1])
    placed = view.at[chosen].set(part.reshape(chosen.shape[0], FR_ROWS, array.shape[1]))
    return placed.reshape(array.shape)

def pick_snapshot(stack, ages):
    blocks = stack.shape[1] // FR_ROWS
    view = stack.reshape(stack.shape[0], blocks, FR_ROWS, stack.shape[2])
    levels = jnp.arange(stack.shape[0], dtype=jnp.int32)
    mask = levels[:, None] == ages[None, :] - 1
    picked = lax.optimization_barrier(jnp.sum(jnp.where(mask[:, :, None, None], view, jnp.zeros_like(view)), axis=0))
    return picked.reshape(stack.shape[1], stack.shape[2])

def inner_step(hidden_raw, incoming, gain, weights_master, moment_one, moment_two):
    out_scale = float(D) ** (-0.5)
    hidden_in = hidden_raw.astype(jnp.float32)
    inverse_rms = lax.rsqrt(lax.optimization_barrier(jnp.mean(hidden_in * hidden_in, axis=1, keepdims=True)) + norm_eps)
    unit_rows = hidden_in * inverse_rms
    gain_factor = 1.0 + gain
    normed = (unit_rows * gain_factor).astype(jnp.bfloat16)
    weights_bf = weights_master.astype(jnp.bfloat16)
    values = (jnp.dot(normed, weights_bf, preferred_element_type=jnp.float32) * out_scale).astype(jnp.bfloat16)
    gradient = jnp.dot(normed.T, incoming, preferred_element_type=jnp.float32) * out_scale
    dnormed = jnp.dot(incoming, weights_bf.T, preferred_element_type=jnp.float32) * out_scale
    gain_total = lax.optimization_barrier(jnp.sum(dnormed * unit_rows, axis=0))
    scaled_up = dnormed * gain_factor
    input_grad = (inverse_rms * (scaled_up - unit_rows * lax.optimization_barrier(jnp.mean(scaled_up * unit_rows, axis=1, keepdims=True)))).astype(jnp.bfloat16)
    first_new = beta_one * moment_one + (1.0 - beta_one) * gradient
    second_new = beta_two * moment_two + (1.0 - beta_two) * gradient * gradient
    stepped = weights_master - inner_rate * (first_new / (jnp.sqrt(second_new) + adam_eps) + weight_decay * weights_master)
    return (values, input_grad, gain_total, stepped, first_new, second_new)

def reference(residual, cotangent, norm_gain, master, first_moment, second_moment, anchor, outer_momentum, history, fragment, delay):
    chosen = block_index(fragment)
    results = [inner_step(residual[index], cotangent[index], norm_gain[index], master[index], first_moment[index], second_moment[index]) for index in range(N_REPLICA)]
    anchor_old = take_part(anchor, chosen)
    momentum_old = take_part(outer_momentum, chosen)
    delta = jnp.zeros_like(anchor_old)
    for index in range(N_REPLICA):
        delta = delta + (anchor_old - pick_snapshot(history[index], delay[index]))
    delta = delta / N_REPLICA
    momentum_part = outer_beta * momentum_old + delta
    anchor_part = anchor_old - outer_rate * (delta + outer_beta * momentum_part)
    new_anchor = put_part(anchor, anchor_part, chosen)
    new_momentum = put_part(outer_momentum, momentum_part, chosen)
    merged = []
    for item in results:
        stepped = item[3]
        mixed = mix_weight * take_part(stepped, chosen) + (1.0 - mix_weight) * anchor_part
        merged.append(put_part(stepped, mixed, chosen))
    values = jnp.stack([item[0] for item in results])
    input_grad = jnp.stack([item[1] for item in results])
    gain_grad = jnp.stack([item[2] for item in results])
    new_first = jnp.stack([item[4] for item in results])
    new_second = jnp.stack([item[5] for item in results])
    return (values, input_grad, gain_grad, jnp.stack(merged), new_first, new_second, new_anchor, new_momentum)
```

```python
import jax
import jax.numpy as jnp
from jax import lax
from jax.experimental import pallas as pl
from jax.experimental.pallas import tpu as pltpu
from jax.sharding import PartitionSpec as P

D = 4608
DV = 1024
FRAGS = 6
FR_ROWS = 8
HIST = 4

T = 256
R = 144
SLOT = 2 * R
ZR = 4 * SLOT
H = 2 * ZR
TILE = 384
NZ = 640
NX = DV - NZ
PART = R // FRAGS
QUART = DV // 4

norm_eps = 1e-06
beta_one = 0.9
beta_two = 0.95
inner_rate = 0.01
weight_decay = 0.1
adam_eps = 1e-08
outer_beta = 0.9
outer_rate = 0.7
mix_weight = 0.5
out_scale = float(D) ** (-0.5)

MESH = pl.DeviceIdType.MESH
F32 = jnp.float32
BF16 = jnp.bfloat16


def main_kernel(
    frag, delay, residual, cotangent, gain, master, anchor, history,
    values_o, igrad_o, ggrad_o, grad_o, delta_o,
    res, resp, cot, gain_v, master_v, anchor_v, hist_v,
    wh, stage, g, normed, inv, dn, vacc, vrecv, vout, rs, rsp, ig, ggx, ggz, ggt,
    opp, full, zbuf, zxbuf, oppx, fullx, oterm, obuf, osum, ozh, od,
    loc, part_s, part_r, agz_s, agz_r, agx_s, agx_r, axx_s, axx_r, axz_s, axz_r,
    rsx_s, rsx_r, rsz_s, rsz_r, rxz_s, rxz_r, rxx_s, rxx_r, gx_s, gx_r, gz_s, gz_r,
    oy_s, oy_r, oz_s, oz_r, ob_s, ob_r,
):
    me = lax.axis_index("fsdp")
    rep = lax.axis_index("replica")
    q, x, c = me // 8, (me // 2) % 4, me % 2
    y, zh = rep // 2, rep % 2
    xr, xl, xo = (x + 1) % 4, (x + 3) % 4, (x + 2) % 4
    handler = c == q // 2
    near = jnp.where(q <= 2 * c, 0, 1)
    far = 1 - near

    def dev(qq, xx, cc):
        return {"fsdp": qq * 8 + xx * 2 + cc}

    partner, right, left = dev(q, x, 1 - c), dev(q, xr, c), dev(q, xl, c)
    up, down = dev(q + 1, x, c), dev(q - 1, x, c)

    sends = []

    def copy(src, dst, send, recv, to):
        return pltpu.make_async_remote_copy(
            src_ref=src, dst_ref=dst, send_sem=send, recv_sem=recv, device_id=to, device_id_type=MESH
        )

    def when(cond, run):
        if cond is None:
            run()
        else:
            @pl.when(cond)
            def _():
                run()

    def go(src, dst, send, recv, to, cond=None):
        made = copy(src, dst, send, recv, to)
        when(cond, lambda: made.start())
        sends.append((cond, made))

    def got(dst, recv, cond=None):
        made = copy(dst, dst, part_s.at[0], recv, partner)
        when(cond, lambda: made.wait_recv())

    local_in = [
        pltpu.make_async_copy(master.at[0], master_v, loc.at[0]),
        pltpu.make_async_copy(residual.at[0], res, loc.at[1]),
        pltpu.make_async_copy(cotangent.at[0], cot.at[pl.ds(0, T)], loc.at[2]),
        pltpu.make_async_copy(gain, gain_v, loc.at[3]),
        pltpu.make_async_copy(anchor, anchor_v, loc.at[4]),
        pltpu.make_async_copy(history.at[0], hist_v, loc.at[5]),
    ]
    for item in local_in:
        item.start()

    barrier = pltpu.get_barrier_semaphore()
    greeted = [partner]
    greeted += [dev(q, (x + k) % 4, c) for k in range(1, 4)]
    greeted += [dev((q + k) % 4, x, c) for k in range(1, 4)]
    greeted += [{"replica": ((y + k) % 4) * 2 + zh} for k in range(1, 4)]
    greeted += [{"replica": y * 2 + 1 - zh}]
    for to in greeted:
        pl.semaphore_signal(barrier, inc=1, device_id=to, device_id_type=MESH)
    pl.semaphore_wait(barrier, len(greeted))

    zcols, xcols = pl.ds(0, NZ), pl.ds(NZ, NX)

    def rows(zl, xx, half=0):
        return pl.multiple_of(zl * ZR + xx * SLOT + half * R, 16)

    def block(buf, zl, xx, cols, half=None):
        if half is None:
            return buf.at[pl.ds(rows(zl, xx), SLOT), cols]
        return buf.at[pl.ds(rows(zl, xx, half), R), cols]

    hcol = pl.multiple_of(c * H, 128)
    pcol = pl.multiple_of((1 - c) * H, 128)

    go(residual.at[0, :, pl.ds(pcol, H)], resp, part_s.at[1], part_r.at[1], partner)
    go(cotangent.at[0], cot.at[pl.ds(T, T)], part_s.at[2], part_r.at[2], partner)

    own = q % 2
    local_in[0].wait()
    own_rows = pl.ds(pl.multiple_of(own * ZR + x * SLOT + c * R, 16), R)

    @pl.when(handler)
    def _():
        wh[own_rows, :] = master_v[...].astype(BF16)

    @pl.when(jnp.logical_not(handler))
    def _():
        stage[...] = master_v[...].astype(BF16)

    go(stage, wh.at[own_rows, :], part_s.at[0], part_r.at[0], partner, jnp.logical_not(handler))
    other_rows = pl.ds(pl.multiple_of(own * ZR + x * SLOT + (1 - c) * R, 16), R)
    got(wh.at[other_rows, :], part_r.at[0], handler)

    def ag_z(zl, cond_extra=None):
        target = 2 * c + zl
        ref = block(wh, zl, x, zcols)
        got(ref, agz_r.at[zl], q != target)
        go(ref, ref, agz_s.at[zl, 0], agz_r.at[zl], up, jnp.logical_and(q >= target, q < 3))
        go(ref, ref, agz_s.at[zl, 1], agz_r.at[zl], down, jnp.logical_and(q <= target, q > 0))

    def ag_x(zl):
        ref = block(wh, zl, x, zcols)
        go(ref, ref, agx_s.at[zl, 0], agx_r.at[zl, 0], right)
        go(ref, ref, agx_s.at[zl, 1], agx_r.at[zl, 1], left)

    def ag_fwd(zl):
        got(block(wh, zl, xl, zcols), agx_r.at[zl, 0])
        ref = block(wh, zl, xl, zcols, 0)
        go(ref, ref, agx_s.at[zl, 2], agx_r.at[zl, 2], right)
        got(block(wh, zl, xr, zcols), agx_r.at[zl, 1])
        ref = block(wh, zl, xr, zcols, 1)
        go(ref, ref, agx_s.at[zl, 3], agx_r.at[zl, 3], left)

    def ag_end(zl):
        got(block(wh, zl, xo, zcols, 0), agx_r.at[zl, 2])
        got(block(wh, zl, xo, zcols, 1), agx_r.at[zl, 3])

    def agx_zsend(zl, slots):
        target = 2 * c + zl
        for k in slots:
            xx = (x, xl, xr, xo)[k]
            ref = block(wh, zl, xx, xcols)
            got(ref, axz_r.at[zl, k], q != target)
            go(ref, ref, axz_s.at[zl, k, 0], axz_r.at[zl, k], up, jnp.logical_and(q >= target, q < 3))
            go(ref, ref, axz_s.at[zl, k, 1], axz_r.at[zl, k], down, jnp.logical_and(q <= target, q > 0))

    if NX:
        ref = block(wh, own, x, xcols)
        go(ref, ref, axx_s.at[0], axx_r.at[0], right, handler)
        go(ref, ref, axx_s.at[1], axx_r.at[1], left, handler)

    target = 2 * c + near
    ref = block(wh, near, x, zcols)
    go(ref, ref, agz_s.at[near, 0], agz_r.at[near], up, jnp.logical_and(handler, q < 3))
    go(ref, ref, agz_s.at[near, 1], agz_r.at[near], down, jnp.logical_and(handler, q > 0))

    def norm_rows(i, _):
        spot = pl.ds(pl.multiple_of(i * 16, 16), 16)
        raw = res[spot, :].astype(F32)
        scale = lax.rsqrt(jnp.mean(raw * raw, axis=1, keepdims=True) + norm_eps)
        inv[spot, :] = jnp.broadcast_to(scale, (16, 128))
        return 0

    local_in[1].wait()
    lax.fori_loop(0, T // 16, norm_rows, 0)
    inv_own = inv.at[pl.ds(0, T)]
    inv_other = inv.at[pl.ds(T, T)]
    go(inv_own, inv_other, part_s.at[3], part_r.at[3], partner)

    if NX:
        got(block(wh, own, xl, xcols), axx_r.at[0], handler)
        ref = block(wh, own, xl, xcols, 0)
        go(ref, ref, axx_s.at[2], axx_r.at[2], right, handler)
        got(block(wh, own, xr, xcols), axx_r.at[1], handler)
        ref = block(wh, own, xr, xcols, 1)
        go(ref, ref, axx_s.at[3], axx_r.at[3], left, handler)

        def agx_own(slots):
            for k in slots:
                xx = (x, xl, xr, xo)[k]
                ref = block(wh, near, xx, xcols)
                go(ref, ref, axz_s.at[near, k, 0], axz_r.at[near, k], up, jnp.logical_and(handler, q < 3))
                go(ref, ref, axz_s.at[near, k, 1], axz_r.at[near, k], down, jnp.logical_and(handler, q > 0))

        agx_own((0, 1, 2))

    ref = block(wh, near, x, zcols)
    go(ref, ref, agx_s.at[near, 0], agx_r.at[near, 0], right, handler)
    go(ref, ref, agx_s.at[near, 1], agx_r.at[near, 1], left, handler)

    local_in[3].wait()

    def normed_rows(source, col, base):
        def run(i, _):
            spot = pl.ds(pl.multiple_of(i * 16, 16), 16)
            there = pl.ds(pl.multiple_of(base + i * 16, 16), 16)
            scale = inv[there, :][:, :1]
            factor = 1.0 + gain_v[:, pl.ds(hcol, H)]
            raw = source[spot, pl.ds(col, H)].astype(F32)
            normed[there, :] = (raw * scale * factor).astype(BF16)
            return 0

        lax.fori_loop(0, T // 16, run, 0)

    normed_rows(res, hcol, 0)

    far_node = jnp.logical_not(handler)
    if NX:
        got(block(wh, own, xo, xcols, 0), axx_r.at[2], handler)
        got(block(wh, own, xo, xcols, 1), axx_r.at[3], handler)
        agx_own((3,))

    ref = block(wh, near, x, zcols)
    target = 2 * c + near
    got(ref, agz_r.at[near], far_node)
    go(ref, ref, agz_s.at[near, 0], agz_r.at[near], up, jnp.logical_and(far_node, jnp.logical_and(q >= target, q < 3)))
    go(ref, ref, agz_s.at[near, 1], agz_r.at[near], down, jnp.logical_and(far_node, jnp.logical_and(q <= target, q > 0)))
    go(ref, ref, agx_s.at[near, 0], agx_r.at[near, 0], right, far_node)
    go(ref, ref, agx_s.at[near, 1], agx_r.at[near, 1], left, far_node)

    got(inv_other, part_r.at[3])
    got(resp, part_r.at[1])
    normed_rows(resp, 0, T)

    local_in[2].wait()
    got(cot.at[pl.ds(T, T)], part_r.at[2])

    def grad_rows(zl):
        def run(t, _):
            at = zl * ZR + t * TILE
            a = normed[:, pl.ds(pl.multiple_of(at, 128), TILE)]
            part = lax.dot_general(a, cot[...], (((0,), (0,)), ((), ())), preferred_element_type=F32)
            g[pl.ds(pl.multiple_of(at, 16), TILE), :] = (part * out_scale).astype(BF16)
            return 0

        lax.fori_loop(0, ZR // TILE, run, 0)

    def add_into(row, count, cols, terms, cond=None):
        step = 48

        def run(i, _):
            spot = pl.ds(pl.multiple_of(row + i * step, 16), step)
            here = pl.ds(pl.multiple_of(i * step, 16), step)
            total = g[spot, cols].astype(F32)
            for term in terms:
                total = total + term[here, :].astype(F32)
            g[spot, cols] = total.astype(BF16)
            return 0

        when(cond, lambda: lax.fori_loop(0, count // step, run, 0))

    def rs_opp(zl):
        go(block(g, zl, xo, zcols, 0), opp.at[zl, 0], rsx_s.at[zl, 0], rsx_r.at[zl, 0], right)
        go(block(g, zl, xo, zcols, 1), opp.at[zl, 1], rsx_s.at[zl, 1], rsx_r.at[zl, 1], left)

    def rs_full(zl):
        got(opp.at[zl, 0], rsx_r.at[zl, 0])
        add_into(rows(zl, xr, 0), R, zcols, [opp.at[zl, 0]])
        go(block(g, zl, xr, zcols), full.at[zl, 0], rsx_s.at[zl, 2], rsx_r.at[zl, 2], right)
        got(opp.at[zl, 1], rsx_r.at[zl, 1])
        add_into(rows(zl, xl, 1), R, zcols, [opp.at[zl, 1]])
        go(block(g, zl, xl, zcols), full.at[zl, 1], rsx_s.at[zl, 3], rsx_r.at[zl, 3], left)

    def rs_z(zl):
        target = 2 * c + zl
        got(full.at[zl, 0], rsx_r.at[zl, 2])
        got(full.at[zl, 1], rsx_r.at[zl, 3])
        add_into(rows(zl, x), SLOT, zcols, [full.at[zl, 0], full.at[zl, 1]])
        above = jnp.logical_and(q >= target, q < 3)
        below = jnp.logical_and(q <= target, q > 0)
        got(zbuf.at[zl, 1], rsz_r.at[zl, 1], above)
        add_into(rows(zl, x), SLOT, zcols, [zbuf.at[zl, 1]], above)
        got(zbuf.at[zl, 0], rsz_r.at[zl, 0], below)
        add_into(rows(zl, x), SLOT, zcols, [zbuf.at[zl, 0]], below)
        ref = block(g, zl, x, zcols)
        go(ref, zbuf.at[zl, 1], rsz_s.at[zl, 0], rsz_r.at[zl, 1], down, q > target)
        go(ref, zbuf.at[zl, 0], rsz_s.at[zl, 1], rsz_r.at[zl, 0], up, q < target)

    def rsx_z(zl, slots=(3, 1, 2, 0)):
        target = 2 * c + zl
        above = jnp.logical_and(q >= target, q < 3)
        below = jnp.logical_and(q <= target, q > 0)
        for k in slots:
            xx = (x, xl, xr, xo)[k]
            got(zxbuf.at[zl, 1, k], rxz_r.at[zl, 1, k], above)
            add_into(rows(zl, xx), SLOT, xcols, [zxbuf.at[zl, 1, k]], above)
            got(zxbuf.at[zl, 0, k], rxz_r.at[zl, 0, k], below)
            add_into(rows(zl, xx), SLOT, xcols, [zxbuf.at[zl, 0, k]], below)
            ref = block(g, zl, xx, xcols)
            go(ref, zxbuf.at[zl, 1, k], rxz_s.at[zl, 0, k], rxz_r.at[zl, 1, k], down, q > target)
            go(ref, zxbuf.at[zl, 0, k], rxz_s.at[zl, 1, k], rxz_r.at[zl, 0, k], up, q < target)

    def outer_start():
        local_in[4].wait()
        local_in[5].wait()
        for b in range(R // (FRAGS * FR_ROWS)):
            first = me * (R // FR_ROWS) + b * FRAGS
            spot = pl.ds(b * FR_ROWS, FR_ROWS)
            term = jnp.zeros((FR_ROWS, DV), F32)
            for k in range(FRAGS):
                taken = (frag[first + k] == 0).astype(F32)
                term = term + taken * anchor_v[pl.ds((b * FRAGS + k) * FR_ROWS, FR_ROWS), :]
            for k in range(HIST):
                taken = (delay[0, b] == k + 1).astype(F32)
                term = term - taken * hist_v[k, spot, :]
            oterm[spot, :] = term
        obuf[y] = oterm[:, pl.ds(pl.multiple_of(y * QUART, 128), QUART)]
        for k in range(1, 4):
            yy = (y + k) % 4
            go(
                oterm.at[:, pl.ds(pl.multiple_of(yy * QUART, 128), QUART)], obuf.at[y],
                oy_s.at[k], oy_r.at[k], {"replica": yy * 2 + zh},
            )

    def outer_mid():
        for k in range(1, 4):
            got(obuf.at[(y + 4 - k) % 4], oy_r.at[k])
        osum[...] = (obuf[0] + obuf[1]) + (obuf[2] + obuf[3])
        go(osum, ozh, oz_s, oz_r, {"replica": y * 2 + 1 - zh})

    def outer_last():
        got(ozh, oz_r)
        mine = pl.ds(pl.multiple_of(y * QUART, 128), QUART)
        od[:, mine] = (osum[...] + ozh[...]) * 0.125
        for k in range(1, 4):
            go(od.at[:, mine], od.at[:, mine], ob_s.at[k], ob_r.at[k], {"replica": ((y + k) % 4) * 2 + zh})

    def outer_out():
        for k in range(1, 4):
            theirs = pl.ds(pl.multiple_of(((y + 4 - k) % 4) * QUART, 128), QUART)
            got(od.at[:, theirs], ob_r.at[k])

    def near_far_values(zl, first):
        def run(n, _):
            cols = pl.ds(pl.multiple_of(n * 256, 128), 256)
            part = jnp.dot(
                normed[:, pl.ds(pl.multiple_of(zl * ZR, 128), ZR)],
                wh[pl.ds(pl.multiple_of(zl * ZR, 16), ZR), cols],
                preferred_element_type=F32,
            )
            if first:
                vacc[:, cols] = part
            else:
                vacc[:, cols] = vacc[:, cols] + part
            return 0

        lax.fori_loop(0, DV // 256, run, 0)

    def dnormed(zl):
        def run(t, _):
            at = zl * ZR + t * TILE
            part = lax.dot_general(
                cot[...], wh[pl.ds(pl.multiple_of(at, 16), TILE), :], (((1,), (1,)), ((), ())),
                preferred_element_type=F32,
            )
            dn[:, pl.ds(pl.multiple_of(at, 128), TILE)] = part * out_scale
            return 0

        lax.fori_loop(0, ZR // TILE, run, 0)

    def sums(zl, first):
        at = pl.multiple_of(zl * ZR, 128)
        factor = 1.0 + gain_v[:, pl.ds(pl.multiple_of(hcol + at, 128), ZR)]

        def part_of(source, col, base, total):
            def run(i, total):
                spot = pl.ds(pl.multiple_of(i * 16, 16), 16)
                there = pl.ds(pl.multiple_of(base + i * 16, 16), 16)
                unit = source[spot, pl.ds(col, ZR)].astype(F32) * inv[there, :][:, :1]
                prod = dn[there, pl.ds(at, ZR)] * unit
                scaled = prod * factor
                lanes = scaled[:, :128]
                for k in range(1, ZR // 128):
                    lanes = lanes + scaled[:, k * 128 : (k + 1) * 128]
                if first:
                    rs[there, :] = lanes
                else:
                    rs[there, :] = rs[there, :] + lanes
                return total + (prod[:8] + prod[8:])

            return lax.fori_loop(0, T // 16, run, total)

        total = jnp.zeros((8, ZR), F32)
        total = part_of(res, pl.multiple_of(hcol + at, 128), 0, total)
        total = part_of(resp, at, T, total)
        ggt[:, pl.ds(at, ZR)] = jnp.sum(total, axis=0, keepdims=True)

    def input_grad(source, col, base):
        factor = 1.0 + gain_v[:, pl.ds(hcol, H)]

        def run(i, _):
            spot = pl.ds(pl.multiple_of(i * 16, 16), 16)
            there = pl.ds(pl.multiple_of(base + i * 16, 16), 16)
            scale = inv[there, :][:, :1]
            unit = source[spot, pl.ds(col, H)].astype(F32) * scale
            there_too = pl.ds(pl.multiple_of(T - base + i * 16, 16), 16)
            mean = jnp.sum(rs[there, :] + rsp[there_too, :], axis=1, keepdims=True) * (1.0 / D)
            ig[there, :] = (scale * (dn[there, :] * factor - unit * mean)).astype(BF16)
            return 0

        lax.fori_loop(0, T // 16, run, 0)

    grad_rows(far)
    rs_opp(far)
    ag_fwd(near)
    grad_rows(near)
    rs_opp(near)
    if NX:
        rsx_z(far)
    rs_full(far)
    outer_start()
    if NX:
        target = 2 * c + near
        for k in range(4):
            xx = (x, xl, xr, xo)[k]
            ref = block(wh, near, xx, xcols)
            got(ref, axz_r.at[near, k], far_node)
            go(ref, ref, axz_s.at[near, k, 0], axz_r.at[near, k], up,
               jnp.logical_and(far_node, jnp.logical_and(q >= target, q < 3)))
            go(ref, ref, axz_s.at[near, k, 1], axz_r.at[near, k], down,
               jnp.logical_and(far_node, jnp.logical_and(q <= target, q > 0)))
    ag_z(far)
    ag_x(far)
    rs_full(near)
    if NX:
        rsx_z(near)
    outer_mid()
    ag_fwd(far)
    rs_z(far)
    if NX:
        agx_zsend(far, range(4))
    outer_last()
    ag_end(near)
    near_far_values(near, True)
    dnormed(near)
    rs_z(near)

    def rs_last():
        if NX:
            go(block(g, own, xo, xcols, 0), oppx.at[0], rxx_s.at[0], rxx_r.at[0], right, handler)
            go(block(g, own, xo, xcols, 1), oppx.at[1], rxx_s.at[1], rxx_r.at[1], left, handler)

    rs_last()
    sums(near, True)
    if NX:
        got(oppx.at[0], rxx_r.at[0], handler)
        add_into(rows(own, xr, 0), R, xcols, [oppx.at[0]], handler)
        go(block(g, own, xr, xcols), fullx.at[0], rxx_s.at[2], rxx_r.at[2], right, handler)
        got(oppx.at[1], rxx_r.at[1], handler)
        add_into(rows(own, xl, 1), R, xcols, [oppx.at[1]], handler)
        go(block(g, own, xl, xcols), fullx.at[1], rxx_s.at[3], rxx_r.at[3], left, handler)
    outer_out()
    delta_out = pltpu.make_async_copy(od, delta_o, loc.at[6])
    delta_out.start()

    ag_end(far)
    near_far_values(far, False)
    other_tokens = pl.ds(T, T)
    go(vacc.at[other_tokens], vrecv, part_s.at[4], part_r.at[4], partner)
    dnormed(far)
    sums(far, False)
    go(rs, rsp, part_s.at[5], part_r.at[5], partner)
    ggx[x] = ggt[...]
    for k in range(1, 4):
        go(ggx.at[x], ggx.at[x], gx_s.at[k], gx_r.at[k], dev(q, (x + k) % 4, c))
    got(rsp, part_r.at[5])
    input_grad(resp, 0, T)
    go(ig.at[other_tokens], igrad_o.at[0, :, pl.ds(hcol, H)], part_s.at[6], part_r.at[6], partner)
    for k in range(1, 4):
        got(ggx.at[(x + 4 - k) % 4], gx_r.at[k])
    ggz[q] = (ggx[0] + ggx[1]) + (ggx[2] + ggx[3])
    for k in range(1, 4):
        go(ggz.at[q], ggz.at[q], gz_s.at[k], gz_r.at[k], dev((q + k) % 4, x, c))
    input_grad(res, hcol, 0)
    ig_out = pltpu.make_async_copy(ig.at[pl.ds(0, T)], igrad_o.at[0, :, pl.ds(hcol, H)], loc.at[7])
    ig_out.start()
    got(vrecv, part_r.at[4])
    vout[...] = ((vacc[pl.ds(0, T), :] + vrecv[...]) * out_scale).astype(BF16)
    values_out = pltpu.make_async_copy(vout, values_o.at[0], loc.at[8])
    values_out.start()
    for k in range(1, 4):
        got(ggz.at[(q + 4 - k) % 4], gz_r.at[k])
    ggt[...] = (ggz[0] + ggz[1]) + (ggz[2] + ggz[3])
    gg_out = pltpu.make_async_copy(ggt, ggrad_o.at[:, pl.ds(hcol, H)], loc.at[9])
    gg_out.start()
    go(ggt, ggrad_o.at[:, pl.ds(hcol, H)], part_s.at[7], part_r.at[7], partner)

    if NX:
        got(fullx.at[0], rxx_r.at[2], handler)
        got(fullx.at[1], rxx_r.at[3], handler)
        add_into(rows(own, x), SLOT, xcols, [fullx.at[0], fullx.at[1]], handler)

    grad_mine = pltpu.make_async_copy(g.at[own_rows, :], grad_o, loc.at[10])
    when(handler, lambda: grad_mine.start())
    go(g.at[other_rows, :], grad_o, part_s.at[8], part_r.at[8], partner, handler)
    got(grad_o, part_r.at[8], far_node)
    got(igrad_o.at[0, :, pl.ds(pcol, H)], part_r.at[6])
    got(ggrad_o.at[:, pl.ds(pcol, H)], part_r.at[7])

    when(handler, lambda: grad_mine.wait())
    for item in (delta_out, ig_out, values_out, gg_out):
        item.wait()
    for cond, made in sends:
        when(cond, lambda made=made: made.wait_send())


def main_call(frag, delay, residual, cotangent, gain, master, anchor, history):
    any_space = pl.BlockSpec(memory_space=pl.ANY)
    smem = pl.BlockSpec(memory_space=pltpu.SMEM)
    vm = pltpu.VMEM
    dma = pltpu.SemaphoreType.DMA
    nx = max(NX, 128)
    scratch = [
        vm((T, D), BF16), vm((T, H), BF16), vm((2 * T, DV), BF16), vm((1, D), F32),
        vm((R, DV), F32), vm((R, DV), F32), vm((HIST, PART, DV), F32),
        vm((H, DV), BF16), vm((R, DV), BF16), vm((H, DV), BF16), vm((2 * T, H), BF16),
        vm((2 * T, 128), F32), vm((2 * T, H), F32), vm((2 * T, DV), F32), vm((T, DV), F32),
        vm((T, DV), BF16), vm((2 * T, 128), F32), vm((2 * T, 128), F32), vm((2 * T, H), BF16),
        vm((4, 1, H), F32), vm((4, 1, H), F32), vm((1, H), F32),
        vm((2, 2, R, NZ), BF16), vm((2, 2, SLOT, NZ), BF16), vm((2, 2, SLOT, NZ), BF16),
        vm((2, 2, 4, SLOT, nx), BF16), vm((2, R, nx), BF16), vm((2, SLOT, nx), BF16),
        vm((PART, DV), F32), vm((4, PART, QUART), F32), vm((PART, QUART), F32),
        vm((PART, QUART), F32), vm((PART, DV), F32),
        dma((11,)), dma((9,)), dma((9,)), dma((2, 2)), dma((2,)), dma((2, 4)), dma((2, 4)),
        dma((4,)), dma((4,)), dma((2, 4, 2)), dma((2, 4)),
        dma((2, 4)), dma((2, 4)), dma((2, 2)), dma((2, 2)),
        dma((2, 2, 4)), dma((2, 2, 4)), dma((4,)), dma((4,)),
        dma((4,)), dma((4,)), dma((4,)), dma((4,)),
        dma((4,)), dma((4,)), dma, dma, dma((4,)), dma((4,)),
    ]
    return pl.pallas_call(
        main_kernel,
        out_shape=(
            jax.ShapeDtypeStruct((1, T, DV), BF16),
            jax.ShapeDtypeStruct((1, T, D), BF16),
            jax.ShapeDtypeStruct((1, D), F32),
            jax.ShapeDtypeStruct((R, DV), BF16),
            jax.ShapeDtypeStruct((PART, DV), F32),
        ),
        in_specs=[smem, smem] + [any_space] * 6,
        out_specs=(any_space,) * 5,
        scratch_shapes=scratch,
        compiler_params=pltpu.CompilerParams(
            collective_id=0, has_side_effects=True, vmem_limit_bytes=52 * 1024 * 1024
        ),
        name="inner_step",
    )(frag, delay, residual, cotangent, gain, master, anchor, history)


def update_kernel(frag, grad, master, first, second, anchor, momentum, delta,
                  master_o, first_o, second_o, anchor_o, momentum_o):
    group = pl.program_id(0)
    start = lax.axis_index("fsdp") * (R // FR_ROWS) + group * FRAGS
    chosen = jnp.int32(0)
    for k in range(1, FRAGS):
        chosen = chosen + jnp.where(frag[start + k] == 0, k, 0)
    at = pl.ds(pl.multiple_of(chosen * FR_ROWS, FR_ROWS), FR_ROWS)

    gradient = grad[...].astype(F32)
    weights = master[0]
    first_new = beta_one * first[0] + (1.0 - beta_one) * gradient
    second_new = beta_two * second[0] + (1.0 - beta_two) * gradient * gradient
    first_o[0] = first_new
    second_o[0] = second_new
    master_o[0] = weights - inner_rate * (
        first_new / (jnp.sqrt(second_new) + adam_eps) + weight_decay * weights
    )

    change = delta[...]
    anchor_old = anchor[at, :]
    momentum_part = outer_beta * momentum[at, :] + change
    anchor_part = anchor_old - outer_rate * (change + outer_beta * momentum_part)
    anchor_o[...] = anchor[...]
    momentum_o[...] = momentum[...]
    anchor_o[at, :] = anchor_part
    momentum_o[at, :] = momentum_part
    master_o[0, at, :] = mix_weight * master_o[0, at, :] + (1.0 - mix_weight) * anchor_part


def update_call(frag, grad, master, first, second, anchor, momentum, delta):
    rows = FRAGS * FR_ROWS
    flat = pl.BlockSpec((rows, DV), lambda i: (i, 0))
    deep = pl.BlockSpec((1, rows, DV), lambda i: (0, i, 0))
    like3 = jax.ShapeDtypeStruct((1, R, DV), F32)
    like2 = jax.ShapeDtypeStruct((R, DV), F32)
    return pl.pallas_call(
        update_kernel,
        grid=(R // rows,),
        out_shape=(like3, like3, like3, like2, like2),
        in_specs=[
            pl.BlockSpec(memory_space=pltpu.SMEM), flat, deep, deep, deep, flat, flat,
            pl.BlockSpec((FR_ROWS, DV), lambda i: (i, 0)),
        ],
        out_specs=(deep, deep, deep, flat, flat),
        name="update",
    )(frag, grad, master, first, second, anchor, momentum, delta)


def body(
    residual, cotangent, norm_gain, master, first_moment, second_moment,
    anchor, outer_momentum, history, fragment, delay,
):
    values, input_grad, gain_grad, gradient, delta = main_call(
        fragment, delay, residual, cotangent, norm_gain, master, anchor, history
    )
    new_master, new_first, new_second, new_anchor, new_momentum = update_call(
        fragment, gradient, master, first_moment, second_moment, anchor, outer_momentum, delta
    )
    return (
        values, input_grad, gain_grad, new_master, new_first, new_second, new_anchor, new_momentum,
    )


def solution(mesh):
    rows = P("replica", "fsdp", None)
    both = P("fsdp", None)
    return jax.shard_map(
        body,
        mesh=mesh,
        in_specs=(
            rows, rows, P("replica", None), rows, rows, rows, both, both,
            P("replica", None, "fsdp", None), P(), P("replica", "fsdp"),
        ),
        out_specs=(rows, rows, P("replica", None), rows, rows, rows, both, both),
        check_vma=False,
    )
```

```python
import jax
import jax.numpy as jnp
from jax import lax
from jax.experimental import pallas as pl
from jax.experimental.pallas import tpu as pltpu
from jax.sharding import PartitionSpec as P

D = 4608
DV = 1024
FRAGS = 6
FR_ROWS = 8
HIST = 4

T = 256
R = 144
SLOT = 2 * R
ZR = 4 * SLOT
H = 2 * ZR
TILE = 384
NZ = 640
NX = DV - NZ
PART = R // FRAGS
QUART = DV // 4

norm_eps = 1e-06
beta_one = 0.9
beta_two = 0.95
inner_rate = 0.01
weight_decay = 0.1
adam_eps = 1e-08
outer_beta = 0.9
outer_rate = 0.7
mix_weight = 0.5
out_scale = float(D) ** (-0.5)

MESH = pl.DeviceIdType.MESH
F32 = jnp.float32
BF16 = jnp.bfloat16


ORDERS = [
    [
        0, 1, 3, 11, 7, 2, 5, 4, 8, 51, 31, 6, 32, 10, 9, 53, 13, 33, 19, 12, 65, 52, 66, 67, 20, 64, 54, 40,
        34, 55, 56, 68, 70, 61, 41, 71, 69, 21, 35, 42, 63, 57, 58, 24, 36, 48, 37, 22, 62, 47, 49, 59, 27,
        50, 14, 60, 23, 15, 16, 25, 29, 26, 38, 28, 39, 17, 18,
    ],
    [
        0, 1, 3, 11, 2, 7, 4, 8, 5, 12, 51, 32, 64, 6, 13, 31, 65, 10, 19, 9, 20, 67, 33, 66, 34, 53, 52, 55,
        40, 41, 56, 54, 42, 61, 69, 57, 68, 58, 21, 35, 47, 62, 70, 63, 71, 50, 59, 24, 49, 48, 14, 37, 23,
        36, 25, 60, 15, 16, 27, 26, 38, 22, 17, 29, 39, 18, 28,
    ],
    [
        11, 13, 12, 30, 43, 55, 34, 51, 65, 56, 19, 35, 45, 32, 71, 52, 68, 69, 70, 31, 53, 58, 46, 64, 20,
        57, 44, 67, 37, 66, 47, 50, 36, 33, 49, 54, 48, 21, 40, 42, 59, 61, 63, 38, 60, 41, 24, 62, 39, 23,
        25, 27, 22, 26, 28, 29,
    ],
    [
        11, 19, 13, 12, 55, 68, 56, 69, 34, 71, 70, 58, 35, 48, 50, 57, 49, 47, 30, 43, 51, 20, 32, 45, 31,
        36, 59, 60, 37, 44, 46, 53, 21, 65, 52, 33, 64, 40, 41, 38, 42, 22, 67, 39, 66, 54, 61, 63, 24, 62,
        23, 25, 27, 29, 28, 26,
    ],
]


def step(number, run):
    run()


def main_kernel(
    frag, delay, residual, cotangent, gain, master, anchor, history,
    values_o, igrad_o, ggrad_o, grad_o, delta_o,
    res, resp, cot, gain_v, master_v, anchor_v, hist_v,
    wh, stage, g, normed, inv, dn, vacc, vrecv, vout, rs, rsp, ig, ggx, ggz, ggt,
    opp, full, zbuf, zxbuf, oppx, fullx, oterm, obuf, osum, ozh, od,
    loc, part_s, part_r, agz_s, agz_r, agx_s, agx_r, axx_s, axx_r, axz_s, axz_r,
    rsx_s, rsx_r, rsz_s, rsz_r, rxz_s, rxz_r, rxx_s, rxx_r, gx_s, gx_r, gz_s, gz_r,
    oy_s, oy_r, oz_s, oz_r, ob_s, ob_r,
):
    me = lax.axis_index("fsdp")
    rep = lax.axis_index("replica")
    q, x, c = me // 8, (me // 2) % 4, me % 2
    y, zh = rep // 2, rep % 2
    xr, xl, xo = (x + 1) % 4, (x + 3) % 4, (x + 2) % 4
    handler = c == q // 2
    place = jnp.where(c == 0, q, 3 - q)
    near = jnp.where(place == 0, c, 1 - c)
    far = 1 - near

    def dev(qq, xx, cc):
        return {"fsdp": qq * 8 + xx * 2 + cc}

    partner, right, left = dev(q, x, 1 - c), dev(q, xr, c), dev(q, xl, c)
    up, down = dev(q + 1, x, c), dev(q - 1, x, c)

    sends = []

    def copy(src, dst, send, recv, to):
        return pltpu.make_async_remote_copy(
            src_ref=src, dst_ref=dst, send_sem=send, recv_sem=recv, device_id=to, device_id_type=MESH
        )

    def when(cond, run):
        if cond is True:
            run()
        elif cond is not False:
            @pl.when(cond)
            def _():
                run()

    def go(src, dst, send, recv, to, cond=True):
        made = copy(src, dst, send, recv, to)
        when(cond, lambda: made.start())
        sends.append((cond, made))

    def got(dst, recv, cond=True):
        made = copy(dst, dst, part_s.at[0], recv, partner)
        when(cond, lambda: made.wait_recv())

    local_in = [
        pltpu.make_async_copy(master.at[0], master_v, loc.at[0]),
        pltpu.make_async_copy(residual.at[0], res, loc.at[1]),
        pltpu.make_async_copy(cotangent.at[0], cot.at[pl.ds(0, T)], loc.at[2]),
        pltpu.make_async_copy(gain, gain_v, loc.at[3]),
        pltpu.make_async_copy(anchor, anchor_v, loc.at[4]),
        pltpu.make_async_copy(history.at[0], hist_v, loc.at[5]),
    ]
    for item in local_in:
        item.start()

    barrier = pltpu.get_barrier_semaphore()
    greeted = [partner]
    greeted += [dev(q, (x + k) % 4, c) for k in range(1, 4)]
    greeted += [dev((q + k) % 4, x, c) for k in range(1, 4)]
    greeted += [{"replica": ((y + k) % 4) * 2 + zh} for k in range(1, 4)]
    greeted += [{"replica": y * 2 + 1 - zh}]
    for to in greeted:
        pl.semaphore_signal(barrier, inc=1, device_id=to, device_id_type=MESH)
    pl.semaphore_wait(barrier, len(greeted))

    zcols, xcols = pl.ds(0, NZ), pl.ds(NZ, NX)

    def rows(zl, xx, half=0):
        return pl.multiple_of(zl * ZR + xx * SLOT + half * R, 16)

    def block(buf, zl, xx, cols, half=None):
        if half is None:
            return buf.at[pl.ds(rows(zl, xx), SLOT), cols]
        return buf.at[pl.ds(rows(zl, xx, half), R), cols]

    hcol = pl.multiple_of(c * H, 128)
    pcol = pl.multiple_of((1 - c) * H, 128)

    own = q % 2
    local_in[0].wait()
    own_rows = pl.ds(pl.multiple_of(own * ZR + x * SLOT + c * R, 16), R)

    @pl.when(handler)
    def _():
        wh[own_rows, :] = master_v[...].astype(BF16)

    @pl.when(jnp.logical_not(handler))
    def _():
        stage[...] = master_v[...].astype(BF16)

    go(stage, wh.at[own_rows, :], part_s.at[0], part_r.at[0], partner, jnp.logical_not(handler))
    other_rows = pl.ds(pl.multiple_of(own * ZR + x * SLOT + (1 - c) * R, 16), R)

    go(residual.at[0, :, pl.ds(pcol, H)], resp, part_s.at[1], part_r.at[1], partner)
    go(cotangent.at[0], cot.at[pl.ds(T, T)], part_s.at[2], part_r.at[2], partner)

    first_sends = len(sends)

    def all_steps(owner, order):
        def slot_of(k):
            return (x, xl, xr, xo)[k]

        def towards(zl):
            goal = 2 * c + zl
            return jnp.logical_and(q >= goal, q < 3), jnp.logical_and(q <= goal, q > 0)

        def both(fixed, cond):
            return cond if fixed else False

        def own_in():
            got(wh.at[other_rows, :], part_r.at[0], owner)

        def ag_z_send(zl, cond):
            ref = block(wh, zl, x, zcols)
            go_up, go_down = towards(zl)
            go(ref, ref, agz_s.at[zl, 0], agz_r.at[zl], up, both(cond, go_up))
            go(ref, ref, agz_s.at[zl, 1], agz_r.at[zl], down, both(cond, go_down))

        def ag_x_send(zl, cond):
            ref = block(wh, zl, x, zcols)
            go(ref, ref, agx_s.at[zl, 0], agx_r.at[zl, 0], right, cond)
            go(ref, ref, agx_s.at[zl, 1], agx_r.at[zl, 1], left, cond)

        def ag_z(zl):
            cond = not (owner and zl is near)
            got(block(wh, zl, x, zcols), agz_r.at[zl], cond)
            ag_z_send(zl, cond)
            ag_x_send(zl, cond)

        def ag_left(zl):
            got(block(wh, zl, xl, zcols), agx_r.at[zl, 0])
            ref = block(wh, zl, xl, zcols, 0)
            go(ref, ref, agx_s.at[zl, 2], agx_r.at[zl, 2], right)

        def ag_right(zl):
            got(block(wh, zl, xr, zcols), agx_r.at[zl, 1])
            ref = block(wh, zl, xr, zcols, 1)
            go(ref, ref, agx_s.at[zl, 3], agx_r.at[zl, 3], left)

        def ag_end(zl):
            got(block(wh, zl, xo, zcols, 0), agx_r.at[zl, 2])
            got(block(wh, zl, xo, zcols, 1), agx_r.at[zl, 3])

        def ax_send():
            ref = block(wh, own, x, xcols)
            go(ref, ref, axx_s.at[0], axx_r.at[0], right, owner)
            go(ref, ref, axx_s.at[1], axx_r.at[1], left, owner)

        def ax_left():
            got(block(wh, own, xl, xcols), axx_r.at[0], owner)
            ref = block(wh, own, xl, xcols, 0)
            go(ref, ref, axx_s.at[2], axx_r.at[2], right, owner)

        def ax_right():
            got(block(wh, own, xr, xcols), axx_r.at[1], owner)
            ref = block(wh, own, xr, xcols, 1)
            go(ref, ref, axx_s.at[3], axx_r.at[3], left, owner)

        def ax_end():
            got(block(wh, own, xo, xcols, 0), axx_r.at[2], owner)
            got(block(wh, own, xo, xcols, 1), axx_r.at[3], owner)

        def ax_z_send(zl, k, cond):
            ref = block(wh, zl, slot_of(k), xcols)
            go_up, go_down = towards(zl)
            go(ref, ref, axz_s.at[zl, k, 0], axz_r.at[zl, k], up, both(cond, go_up))
            go(ref, ref, axz_s.at[zl, k, 1], axz_r.at[zl, k], down, both(cond, go_down))

        def ax_own(k):
            ax_z_send(near, k, owner)

        def ax_z(zl, k):
            cond = not (owner and zl is near)
            got(block(wh, zl, slot_of(k), xcols), axz_r.at[zl, k], cond)
            ax_z_send(zl, k, cond)

        def norm_rows(i, _):
            spot = pl.ds(pl.multiple_of(i * 16, 16), 16)
            raw = res[spot, :].astype(F32)
            scale = lax.rsqrt(jnp.mean(raw * raw, axis=1, keepdims=True) + norm_eps)
            inv[spot, :] = jnp.broadcast_to(scale, (16, 128))
            return 0

        def scales():
            local_in[3].wait()
            local_in[1].wait()
            lax.fori_loop(0, T // 16, norm_rows, 0)
            go(inv.at[pl.ds(0, T)], inv.at[pl.ds(T, T)], part_s.at[3], part_r.at[3], partner)

        def normed_rows(source, col, base):
            def run(i, _):
                spot = pl.ds(pl.multiple_of(i * 16, 16), 16)
                there = pl.ds(pl.multiple_of(base + i * 16, 16), 16)
                scale = inv[there, :][:, :1]
                factor = 1.0 + gain_v[:, pl.ds(hcol, H)]
                raw = source[spot, pl.ds(col, H)].astype(F32)
                normed[there, :] = (raw * scale * factor).astype(BF16)
                return 0

            lax.fori_loop(0, T // 16, run, 0)

        def normed_own():
            normed_rows(res, hcol, 0)

        def normed_other():
            got(inv.at[pl.ds(T, T)], part_r.at[3])
            got(resp, part_r.at[1])
            normed_rows(resp, 0, T)
            local_in[2].wait()
            got(cot.at[pl.ds(T, T)], part_r.at[2])

        def grad_rows(zl):
            def run(t, _):
                at = zl * ZR + t * TILE
                a = normed[:, pl.ds(pl.multiple_of(at, 128), TILE)]
                part = lax.dot_general(a, cot[...], (((0,), (0,)), ((), ())), preferred_element_type=F32)
                g[pl.ds(pl.multiple_of(at, 16), TILE), :] = (part * out_scale).astype(BF16)
                return 0

            lax.fori_loop(0, ZR // TILE, run, 0)

        def add_into(row, count, cols, terms, cond=True):
            step = 48

            def run(i, _):
                spot = pl.ds(pl.multiple_of(row + i * step, 16), step)
                here = pl.ds(pl.multiple_of(i * step, 16), step)
                total = g[spot, cols].astype(F32)
                for term in terms:
                    total = total + term[here, :].astype(F32)
                g[spot, cols] = total.astype(BF16)
                return 0

            when(cond, lambda: lax.fori_loop(0, count // step, run, 0))

        def rs_opp(zl):
            go(block(g, zl, xo, zcols, 0), opp.at[zl, 0], rsx_s.at[zl, 0], rsx_r.at[zl, 0], right)
            go(block(g, zl, xo, zcols, 1), opp.at[zl, 1], rsx_s.at[zl, 1], rsx_r.at[zl, 1], left)

        def rs_right(zl):
            got(opp.at[zl, 0], rsx_r.at[zl, 0])
            add_into(rows(zl, xr, 0), R, zcols, [opp.at[zl, 0]])
            go(block(g, zl, xr, zcols), full.at[zl, 0], rsx_s.at[zl, 2], rsx_r.at[zl, 2], right)

        def rs_left(zl):
            got(opp.at[zl, 1], rsx_r.at[zl, 1])
            add_into(rows(zl, xl, 1), R, zcols, [opp.at[zl, 1]])
            go(block(g, zl, xl, zcols), full.at[zl, 1], rsx_s.at[zl, 3], rsx_r.at[zl, 3], left)

        def rs_x(zl):
            got(full.at[zl, 0], rsx_r.at[zl, 2])
            got(full.at[zl, 1], rsx_r.at[zl, 3])
            add_into(rows(zl, x), SLOT, zcols, [full.at[zl, 0], full.at[zl, 1]])

        def rs_z(zl):
            above, below = towards(zl)
            got(zbuf.at[zl, 1], rsz_r.at[zl, 1], above)
            add_into(rows(zl, x), SLOT, zcols, [zbuf.at[zl, 1]], above)
            got(zbuf.at[zl, 0], rsz_r.at[zl, 0], below)
            add_into(rows(zl, x), SLOT, zcols, [zbuf.at[zl, 0]], below)
            ref = block(g, zl, x, zcols)
            goal = 2 * c + zl
            go(ref, zbuf.at[zl, 1], rsz_s.at[zl, 0], rsz_r.at[zl, 1], down, q > goal)
            go(ref, zbuf.at[zl, 0], rsz_s.at[zl, 1], rsz_r.at[zl, 0], up, q < goal)

        def rx_z(zl, k):
            above, below = towards(zl)
            xx = slot_of(k)
            got(zxbuf.at[zl, 1, k], rxz_r.at[zl, 1, k], above)
            add_into(rows(zl, xx), SLOT, xcols, [zxbuf.at[zl, 1, k]], above)
            got(zxbuf.at[zl, 0, k], rxz_r.at[zl, 0, k], below)
            add_into(rows(zl, xx), SLOT, xcols, [zxbuf.at[zl, 0, k]], below)
            ref = block(g, zl, xx, xcols)
            goal = 2 * c + zl
            go(ref, zxbuf.at[zl, 1, k], rxz_s.at[zl, 0, k], rxz_r.at[zl, 1, k], down, q > goal)
            go(ref, zxbuf.at[zl, 0, k], rxz_s.at[zl, 1, k], rxz_r.at[zl, 0, k], up, q < goal)

        def rx_opp():
            go(block(g, own, xo, xcols, 0), oppx.at[0], rxx_s.at[0], rxx_r.at[0], right, owner)
            go(block(g, own, xo, xcols, 1), oppx.at[1], rxx_s.at[1], rxx_r.at[1], left, owner)

        def rx_right():
            got(oppx.at[0], rxx_r.at[0], owner)
            add_into(rows(own, xr, 0), R, xcols, [oppx.at[0]], owner)
            go(block(g, own, xr, xcols), fullx.at[0], rxx_s.at[2], rxx_r.at[2], right, owner)

        def rx_left():
            got(oppx.at[1], rxx_r.at[1], owner)
            add_into(rows(own, xl, 1), R, xcols, [oppx.at[1]], owner)
            go(block(g, own, xl, xcols), fullx.at[1], rxx_s.at[3], rxx_r.at[3], left, owner)

        def rx_end():
            got(fullx.at[0], rxx_r.at[2], owner)
            got(fullx.at[1], rxx_r.at[3], owner)
            add_into(rows(own, x), SLOT, xcols, [fullx.at[0], fullx.at[1]], owner)

        grad_mine = pltpu.make_async_copy(g.at[own_rows, :], grad_o, loc.at[10])

        def grad_out():
            when(owner, lambda: grad_mine.start())
            go(g.at[other_rows, :], grad_o, part_s.at[8], part_r.at[8], partner, owner)

        def outer_start():
            local_in[4].wait()
            local_in[5].wait()
            for b in range(R // (FRAGS * FR_ROWS)):
                first = me * (R // FR_ROWS) + b * FRAGS
                spot = pl.ds(b * FR_ROWS, FR_ROWS)
                term = jnp.zeros((FR_ROWS, DV), F32)
                for k in range(FRAGS):
                    taken = (frag[first + k] == 0).astype(F32)
                    term = term + taken * anchor_v[pl.ds((b * FRAGS + k) * FR_ROWS, FR_ROWS), :]
                for k in range(HIST):
                    taken = (delay[0, b] == k + 1).astype(F32)
                    term = term - taken * hist_v[k, spot, :]
                oterm[spot, :] = term
            obuf[y] = oterm[:, pl.ds(pl.multiple_of(y * QUART, 128), QUART)]
            for k in range(1, 4):
                yy = (y + k) % 4
                go(
                    oterm.at[:, pl.ds(pl.multiple_of(yy * QUART, 128), QUART)], obuf.at[y],
                    oy_s.at[k], oy_r.at[k], {"replica": yy * 2 + zh},
                )

        def outer_mid():
            for k in range(1, 4):
                got(obuf.at[(y + 4 - k) % 4], oy_r.at[k])
            osum[...] = (obuf[0] + obuf[1]) + (obuf[2] + obuf[3])
            go(osum, ozh, oz_s, oz_r, {"replica": y * 2 + 1 - zh})

        def outer_last():
            got(ozh, oz_r)
            mine = pl.ds(pl.multiple_of(y * QUART, 128), QUART)
            od[:, mine] = (osum[...] + ozh[...]) * 0.125
            for k in range(1, 4):
                go(od.at[:, mine], od.at[:, mine], ob_s.at[k], ob_r.at[k], {"replica": ((y + k) % 4) * 2 + zh})

        def outer_out():
            for k in range(1, 4):
                theirs = pl.ds(pl.multiple_of(((y + 4 - k) % 4) * QUART, 128), QUART)
                got(od.at[:, theirs], ob_r.at[k])

        def near_far_values(zl, first):
            def run(n, _):
                cols = pl.ds(pl.multiple_of(n * 256, 128), 256)
                part = jnp.dot(
                    normed[:, pl.ds(pl.multiple_of(zl * ZR, 128), ZR)],
                    wh[pl.ds(pl.multiple_of(zl * ZR, 16), ZR), cols],
                    preferred_element_type=F32,
                )
                if first:
                    vacc[:, cols] = part
                else:
                    vacc[:, cols] = vacc[:, cols] + part
                return 0

            lax.fori_loop(0, DV // 256, run, 0)

        def dnormed(zl):
            def run(t, _):
                at = zl * ZR + t * TILE
                part = lax.dot_general(
                    cot[...], wh[pl.ds(pl.multiple_of(at, 16), TILE), :], (((1,), (1,)), ((), ())),
                    preferred_element_type=F32,
                )
                dn[:, pl.ds(pl.multiple_of(at, 128), TILE)] = part * out_scale
                return 0

            lax.fori_loop(0, ZR // TILE, run, 0)

        def sums(zl, first):
            at = pl.multiple_of(zl * ZR, 128)
            factor = 1.0 + gain_v[:, pl.ds(pl.multiple_of(hcol + at, 128), ZR)]

            def part_of(source, col, base, total):
                def run(i, total):
                    spot = pl.ds(pl.multiple_of(i * 16, 16), 16)
                    there = pl.ds(pl.multiple_of(base + i * 16, 16), 16)
                    unit = source[spot, pl.ds(col, ZR)].astype(F32) * inv[there, :][:, :1]
                    prod = dn[there, pl.ds(at, ZR)] * unit
                    scaled = prod * factor
                    lanes = scaled[:, :128]
                    for k in range(1, ZR // 128):
                        lanes = lanes + scaled[:, k * 128 : (k + 1) * 128]
                    if first:
                        rs[there, :] = lanes
                    else:
                        rs[there, :] = rs[there, :] + lanes
                    return total + (prod[:8] + prod[8:])

                return lax.fori_loop(0, T // 16, run, total)

            total = jnp.zeros((8, ZR), F32)
            total = part_of(res, pl.multiple_of(hcol + at, 128), 0, total)
            total = part_of(resp, at, T, total)
            ggt[:, pl.ds(at, ZR)] = jnp.sum(total, axis=0, keepdims=True)

        def input_grad(source, col, base):
            factor = 1.0 + gain_v[:, pl.ds(hcol, H)]

            def run(i, _):
                spot = pl.ds(pl.multiple_of(i * 16, 16), 16)
                there = pl.ds(pl.multiple_of(base + i * 16, 16), 16)
                scale = inv[there, :][:, :1]
                unit = source[spot, pl.ds(col, H)].astype(F32) * scale
                there_too = pl.ds(pl.multiple_of(T - base + i * 16, 16), 16)
                mean = jnp.sum(rs[there, :] + rsp[there_too, :], axis=1, keepdims=True) * (1.0 / D)
                ig[there, :] = (scale * (dn[there, :] * factor - unit * mean)).astype(BF16)
                return 0

            lax.fori_loop(0, T // 16, run, 0)

        delta_copy = pltpu.make_async_copy(od, delta_o, loc.at[6])
        ig_copy = pltpu.make_async_copy(ig.at[pl.ds(0, T)], igrad_o.at[0, :, pl.ds(hcol, H)], loc.at[7])
        values_copy = pltpu.make_async_copy(vout, values_o.at[0], loc.at[8])
        gain_copy = pltpu.make_async_copy(ggt, ggrad_o.at[:, pl.ds(hcol, H)], loc.at[9])

        def values_send():
            go(vacc.at[pl.ds(T, T)], vrecv, part_s.at[4], part_r.at[4], partner)

        def sums_send():
            go(rs, rsp, part_s.at[5], part_r.at[5], partner)
            ggx[x] = ggt[...]
            for k in range(1, 4):
                go(ggx.at[x], ggx.at[x], gx_s.at[k], gx_r.at[k], dev(q, (x + k) % 4, c))

        def igrad_other():
            got(rsp, part_r.at[5])
            input_grad(resp, 0, T)
            go(ig.at[pl.ds(T, T)], igrad_o.at[0, :, pl.ds(hcol, H)], part_s.at[6], part_r.at[6], partner)

        def igrad_own():
            input_grad(res, hcol, 0)
            ig_copy.start()

        def gain_x():
            for k in range(1, 4):
                got(ggx.at[(x + 4 - k) % 4], gx_r.at[k])
            ggz[q] = (ggx[0] + ggx[1]) + (ggx[2] + ggx[3])
            for k in range(1, 4):
                go(ggz.at[q], ggz.at[q], gz_s.at[k], gz_r.at[k], dev((q + k) % 4, x, c))

        def gain_z():
            for k in range(1, 4):
                got(ggz.at[(q + 4 - k) % 4], gz_r.at[k])
            ggt[...] = (ggz[0] + ggz[1]) + (ggz[2] + ggz[3])
            gain_copy.start()
            go(ggt, ggrad_o.at[:, pl.ds(hcol, H)], part_s.at[7], part_r.at[7], partner)

        def values_end():
            got(vrecv, part_r.at[4])
            vout[...] = ((vacc[pl.ds(0, T), :] + vrecv[...]) * out_scale).astype(BF16)
            values_copy.start()

        def delta_end():
            outer_out()
            delta_copy.start()

        steps = [
            own_in, lambda: ag_z_send(near, owner), lambda: ag_x_send(near, owner),
            ax_send, ax_left, ax_right, ax_end,
            lambda: ax_own(0), lambda: ax_own(1), lambda: ax_own(2), lambda: ax_own(3),
            scales, normed_own, normed_other,
            rx_opp, rx_right, rx_left, rx_end, grad_out,
            outer_start, outer_mid, outer_last, delta_end,
            values_send, sums_send, igrad_other, igrad_own, gain_x, gain_z, values_end,
        ]
        for zl, first in ((near, True), (far, False)):
            for run in (
                ag_z, ag_left, ag_right, ag_end, grad_rows, rs_opp,
                rs_right, rs_left, rs_x, rs_z, dnormed,
            ):
                steps.append(lambda run=run, zl=zl: run(zl))
            steps.append(lambda zl=zl, first=first: near_far_values(zl, first))
            steps.append(lambda zl=zl, first=first: sums(zl, first))
            for run in (ax_z, rx_z):
                for k in range(4):
                    steps.append(lambda run=run, zl=zl, k=k: run(zl, k))

        def finish():
            got(grad_o, part_r.at[8], not owner)
            got(igrad_o.at[0, :, pl.ds(pcol, H)], part_r.at[6])
            got(ggrad_o.at[:, pl.ds(pcol, H)], part_r.at[7])
            when(owner, lambda: grad_mine.wait())
            for item in (delta_copy, ig_copy, values_copy, gain_copy):
                item.wait()
            for cond, made in sends[first_sends:]:
                when(cond, lambda made=made: made.wait_send())

        for number in order:
            step(number, steps[number])
        step(-1, finish)
        del sends[first_sends:]

    for kind, order in enumerate(ORDERS):
        @pl.when(place == kind)
        def _(owner=kind < 2, order=order):
            all_steps(owner, order)

    for cond, made in sends:
        when(cond, lambda made=made: made.wait_send())


def main_call(frag, delay, residual, cotangent, gain, master, anchor, history):
    any_space = pl.BlockSpec(memory_space=pl.ANY)
    smem = pl.BlockSpec(memory_space=pltpu.SMEM)
    vm = pltpu.VMEM
    dma = pltpu.SemaphoreType.DMA
    nx = max(NX, 128)
    scratch = [
        vm((T, D), BF16), vm((T, H), BF16), vm((2 * T, DV), BF16), vm((1, D), F32),
        vm((R, DV), F32), vm((R, DV), F32), vm((HIST, PART, DV), F32),
        vm((H, DV), BF16), vm((R, DV), BF16), vm((H, DV), BF16), vm((2 * T, H), BF16),
        vm((2 * T, 128), F32), vm((2 * T, H), F32), vm((2 * T, DV), F32), vm((T, DV), F32),
        vm((T, DV), BF16), vm((2 * T, 128), F32), vm((2 * T, 128), F32), vm((2 * T, H), BF16),
        vm((4, 1, H), F32), vm((4, 1, H), F32), vm((1, H), F32),
        vm((2, 2, R, NZ), BF16), vm((2, 2, SLOT, NZ), BF16), vm((2, 2, SLOT, NZ), BF16),
        vm((2, 2, 4, SLOT, nx), BF16), vm((2, R, nx), BF16), vm((2, SLOT, nx), BF16),
        vm((PART, DV), F32), vm((4, PART, QUART), F32), vm((PART, QUART), F32),
        vm((PART, QUART), F32), vm((PART, DV), F32),
        dma((11,)), dma((9,)), dma((9,)), dma((2, 2)), dma((2,)), dma((2, 4)), dma((2, 4)),
        dma((4,)), dma((4,)), dma((2, 4, 2)), dma((2, 4)),
        dma((2, 4)), dma((2, 4)), dma((2, 2)), dma((2, 2)),
        dma((2, 2, 4)), dma((2, 2, 4)), dma((4,)), dma((4,)),
        dma((4,)), dma((4,)), dma((4,)), dma((4,)),
        dma((4,)), dma((4,)), dma, dma, dma((4,)), dma((4,)),
    ]
    return pl.pallas_call(
        main_kernel,
        out_shape=(
            jax.ShapeDtypeStruct((1, T, DV), BF16),
            jax.ShapeDtypeStruct((1, T, D), BF16),
            jax.ShapeDtypeStruct((1, D), F32),
            jax.ShapeDtypeStruct((R, DV), BF16),
            jax.ShapeDtypeStruct((PART, DV), F32),
        ),
        in_specs=[smem, smem] + [any_space] * 6,
        out_specs=(any_space,) * 5,
        scratch_shapes=scratch,
        compiler_params=pltpu.CompilerParams(
            collective_id=0, has_side_effects=True, vmem_limit_bytes=60 * 1024 * 1024
        ),
        name="inner_step",
    )(frag, delay, residual, cotangent, gain, master, anchor, history)


def update_kernel(
    frag, grad, delta, master, first, second, anchor, momentum, values, igrad, ggrad,
    master_o, first_o, second_o, anchor_o, momentum_o, values_o, igrad_o, ggrad_o,
    grad_v, delta_v, master_v, first_v, second_v, anchor_v, momentum_v,
    master_n, first_n, second_n, igrad_v, values_v, ggrad_v, load, load_small, store, through,
):
    rows = FRAGS * FR_ROWS
    groups = R // rows
    spots = [pl.ds(i * rows, rows) for i in range(groups)]
    small = [
        pltpu.make_async_copy(grad, grad_v, load_small.at[0]),
        pltpu.make_async_copy(delta, delta_v, load_small.at[1]),
    ]
    for item in small:
        item.start()
    loads = []
    for i, at in enumerate(spots):
        loads.append([
            pltpu.make_async_copy(src, dst, load.at[i, k])
            for k, (src, dst) in enumerate((
                (master.at[0, at], master_v.at[at]),
                (first.at[0, at], first_v.at[at]),
                (second.at[0, at], second_v.at[at]),
                (anchor.at[at], anchor_v.at[at]),
                (momentum.at[at], momentum_v.at[at]),
            ))
        ])
        for item in loads[-1]:
            item.start()
    half = T // 2
    taken, passed = [], []
    for k, (src, mid, dst) in enumerate((
        (igrad.at[0, :half], igrad_v.at[:half], igrad_o.at[0, :half]),
        (igrad.at[0, half:], igrad_v.at[half:], igrad_o.at[0, half:]),
        (values.at[0], values_v, values_o.at[0]),
        (ggrad, ggrad_v, ggrad_o),
    )):
        taken.append(pltpu.make_async_copy(src, mid, through.at[0, k]))
        passed.append(pltpu.make_async_copy(mid, dst, through.at[1, k]))
        taken[-1].start()
    for item in small:
        item.wait()
    begin = lax.axis_index("fsdp") * (R // FR_ROWS)
    stores = []
    for i, at in enumerate(spots):
        for item in loads[i]:
            item.wait()
        chosen = jnp.int32(0)
        for k in range(1, FRAGS):
            chosen = chosen + jnp.where(frag[begin + i * FRAGS + k] == 0, k, 0)
        block = pl.ds(pl.multiple_of(i * rows + chosen * FR_ROWS, FR_ROWS), FR_ROWS)

        for piece in range(rows // 16):
            part = pl.ds(i * rows + piece * 16, 16)
            gradient = grad_v[part, :].astype(F32)
            weights = master_v[part, :]
            first_new = beta_one * first_v[part, :] + (1.0 - beta_one) * gradient
            second_new = beta_two * second_v[part, :] + (1.0 - beta_two) * gradient * gradient
            first_n[part, :] = first_new
            second_n[part, :] = second_new
            master_n[part, :] = weights - inner_rate * (
                first_new / (jnp.sqrt(second_new) + adam_eps) + weight_decay * weights
            )
        change = delta_v[pl.ds(i * FR_ROWS, FR_ROWS), :]
        anchor_old = anchor_v[block, :]
        momentum_part = outer_beta * momentum_v[block, :] + change
        anchor_part = anchor_old - outer_rate * (change + outer_beta * momentum_part)
        anchor_v[block, :] = anchor_part
        momentum_v[block, :] = momentum_part
        master_n[block, :] = mix_weight * master_n[block, :] + (1.0 - mix_weight) * anchor_part
        for k, (src, dst) in enumerate((
            (master_n.at[at], master_o.at[0, at]),
            (first_n.at[at], first_o.at[0, at]),
            (second_n.at[at], second_o.at[0, at]),
            (anchor_v.at[at], anchor_o.at[at]),
            (momentum_v.at[at], momentum_o.at[at]),
        )):
            item = pltpu.make_async_copy(src, dst, store.at[i, k])
            item.start()
            stores.append(item)
        if i == 0:
            for came, goes in zip(taken, passed):
                came.wait()
                goes.start()
    for item in stores + passed:
        item.wait()


def update_call(frag, grad, delta, master, first, second, anchor, momentum, values, igrad, ggrad):
    any_space = pl.BlockSpec(memory_space=pl.ANY)
    like3 = jax.ShapeDtypeStruct((1, R, DV), F32)
    like2 = jax.ShapeDtypeStruct((R, DV), F32)
    dma = pltpu.SemaphoreType.DMA
    whole = pltpu.VMEM((R, DV), F32)
    groups = R // (FRAGS * FR_ROWS)
    return pl.pallas_call(
        update_kernel,
        out_shape=(
            like3, like3, like3, like2, like2,
            jax.ShapeDtypeStruct((1, T, DV), BF16),
            jax.ShapeDtypeStruct((1, T, D), BF16),
            jax.ShapeDtypeStruct((1, D), F32),
        ),
        in_specs=[pl.BlockSpec(memory_space=pltpu.SMEM)] + [any_space] * 10,
        out_specs=(any_space,) * 8,
        scratch_shapes=[pltpu.VMEM((R, DV), BF16), pltpu.VMEM((PART, DV), F32)]
        + [whole] * 8
        + [pltpu.VMEM((T, D), BF16), pltpu.VMEM((T, DV), BF16), pltpu.VMEM((1, D), F32)]
        + [dma((groups, 5)), dma((2,)), dma((groups, 5)), dma((2, 4))],
        compiler_params=pltpu.CompilerParams(vmem_limit_bytes=60 * 1024 * 1024),
        name="update",
    )(frag, grad, delta, master, first, second, anchor, momentum, values, igrad, ggrad)


def body(
    residual, cotangent, norm_gain, master, first_moment, second_moment,
    anchor, outer_momentum, history, fragment, delay,
):
    values, input_grad, gain_grad, gradient, delta = main_call(
        fragment, delay, residual, cotangent, norm_gain, master, anchor, history
    )
    new_master, new_first, new_second, new_anchor, new_momentum, values, input_grad, gain_grad = update_call(
        fragment, gradient, delta, master, first_moment, second_moment, anchor, outer_momentum,
        values, input_grad, gain_grad,
    )
    return (
        values, input_grad, gain_grad, new_master, new_first, new_second, new_anchor, new_momentum,
    )


def solution(mesh):
    rows = P("replica", "fsdp", None)
    both = P("fsdp", None)
    return jax.shard_map(
        body,
        mesh=mesh,
        in_specs=(
            rows, rows, P("replica", None), rows, rows, rows, both, both,
            P("replica", None, "fsdp", None), P(), P("replica", "fsdp"),
        ),
        out_specs=(rows, rows, P("replica", None), rows, rows, rows, both, both),
        check_vma=False,
    )
```

```python
import jax
import jax.numpy as jnp
from jax import lax
from jax.experimental import pallas as pl
from jax.experimental.pallas import tpu as pltpu
from jax.sharding import PartitionSpec as P

D = 4608
DV = 1024
FRAGS = 6
FR_ROWS = 8
HIST = 4

T = 256
R = 144
SLOT = 2 * R
ZR = 4 * SLOT
H = 2 * ZR
TILE = 384
NZ = 640
NX = DV - NZ
PART = R // FRAGS
QUART = DV // 4

norm_eps = 1e-06
beta_one = 0.9
beta_two = 0.95
inner_rate = 0.01
weight_decay = 0.1
adam_eps = 1e-08
outer_beta = 0.9
outer_rate = 0.7
mix_weight = 0.5
out_scale = float(D) ** (-0.5)

MESH = pl.DeviceIdType.MESH
F32 = jnp.float32
BF16 = jnp.bfloat16


ORDERS = [
    [
        1, 5, 0, 10, 6, 4, 14, 3, 2, 60, 8, 12, 7, 11, 61, 37, 38, 9, 78, 13, 16, 39, 15, 77, 79, 24, 62, 63,
        50, 49, 80, 65, 64, 40, 51, 82, 25, 84, 66, 74, 81, 68, 41, 83, 26, 67, 76, 69, 75, 29, 42, 27, 44,
        70, 56, 43, 57, 71, 32, 73, 72, 58, 59, 17, 30, 28, 18, 19, 20, 46, 31, 33, 48, 34, 45, 47, 22, 21,
        23,
    ],
    [
        1, 5, 24, 0, 6, 2, 10, 4, 60, 8, 7, 11, 3, 14, 12, 61, 16, 78, 15, 37, 38, 9, 25, 13, 77, 79, 40, 39,
        65, 50, 62, 63, 80, 49, 64, 74, 66, 67, 51, 83, 75, 81, 69, 82, 68, 41, 76, 28, 42, 26, 29, 84, 56,
        57, 58, 30, 59, 17, 71, 70, 44, 43, 18, 73, 32, 31, 72, 20, 19, 27, 34, 45, 46, 47, 48, 33, 22, 21,
        23,
    ],
    [
        14, 35, 15, 16, 36, 65, 60, 53, 40, 54, 67, 61, 37, 52, 66, 38, 55, 83, 78, 63, 69, 77, 81, 41, 62,
        39, 24, 58, 68, 79, 82, 57, 49, 42, 80, 51, 84, 50, 43, 44, 56, 25, 71, 59, 64, 73, 74, 76, 45, 70,
        26, 29, 46, 75, 72, 47, 28, 30, 48, 32, 33, 27, 34, 31,
    ],
    [
        14, 15, 16, 40, 41, 65, 66, 83, 84, 24, 35, 25, 57, 43, 69, 81, 36, 58, 82, 67, 68, 56, 38, 54, 60,
        37, 59, 61, 71, 26, 73, 44, 55, 53, 39, 52, 27, 42, 63, 49, 62, 70, 77, 51, 50, 46, 72, 45, 64, 47,
        79, 48, 78, 80, 74, 76, 29, 75, 30, 32, 31, 28, 33, 34,
    ],
]


def step(number, run):
    run()


def main_kernel(
    frag, delay, residual, cotangent, gain, master, anchor, history,
    values_o, igrad_o, ggrad_o, grad_o, delta_o,
    res, resp, cot, gain_v, master_v, anchor_v, hist_v,
    wh, stage, g, normed, inv, dn, vacc, vrecv, vout, rs, rsp, ig, ggx, ggz, ggt,
    opp, full, zbuf, zxbuf, oppx, fullx, oterm, obuf, osum, ozh, od,
    loc, part_s, part_r, agz_s, agz_r, agx_s, agx_r, axx_s, axx_r, axz_s, axz_r,
    rsx_s, rsx_r, rsz_s, rsz_r, rxz_s, rxz_r, rxx_s, rxx_r, gx_s, gx_r, gz_s, gz_r,
    oy_s, oy_r, oz_s, oz_r, ob_s, ob_r,
):
    me = lax.axis_index("fsdp")
    rep = lax.axis_index("replica")
    q, x, c = me // 8, (me // 2) % 4, me % 2
    y, zh = rep // 2, rep % 2
    xr, xl, xo = (x + 1) % 4, (x + 3) % 4, (x + 2) % 4
    handler = c == q // 2
    place = jnp.where(c == 0, q, 3 - q)
    near = jnp.where(place == 0, c, 1 - c)
    far = 1 - near

    def dev(qq, xx, cc):
        return {"fsdp": qq * 8 + xx * 2 + cc}

    partner, right, left = dev(q, x, 1 - c), dev(q, xr, c), dev(q, xl, c)
    up, down = dev(q + 1, x, c), dev(q - 1, x, c)

    sends = []

    def copy(src, dst, send, recv, to):
        return pltpu.make_async_remote_copy(
            src_ref=src, dst_ref=dst, send_sem=send, recv_sem=recv, device_id=to, device_id_type=MESH
        )

    def when(cond, run):
        if cond is True:
            run()
        elif cond is not False:
            @pl.when(cond)
            def _():
                run()

    def go(src, dst, send, recv, to, cond=True):
        made = copy(src, dst, send, recv, to)
        when(cond, lambda: made.start())
        sends.append((cond, made))

    def got(dst, recv, cond=True):
        made = copy(dst, dst, part_s.at[0], recv, partner)
        when(cond, lambda: made.wait_recv())

    local_in = [
        pltpu.make_async_copy(master.at[0], master_v, loc.at[0]),
        pltpu.make_async_copy(residual.at[0], res, loc.at[1]),
        pltpu.make_async_copy(cotangent.at[0], cot.at[pl.ds(0, T)], loc.at[2]),
        pltpu.make_async_copy(gain, gain_v, loc.at[3]),
        pltpu.make_async_copy(anchor, anchor_v, loc.at[4]),
        pltpu.make_async_copy(history.at[0], hist_v, loc.at[5]),
    ]
    for item in local_in:
        item.start()

    barrier = pltpu.get_barrier_semaphore()
    greeted = [partner]
    greeted += [dev(q, (x + k) % 4, c) for k in range(1, 4)]
    greeted += [dev((q + k) % 4, x, c) for k in range(1, 4)]
    greeted += [{"replica": ((y + k) % 4) * 2 + zh} for k in range(1, 4)]
    greeted += [{"replica": y * 2 + 1 - zh}]
    for to in greeted:
        pl.semaphore_signal(barrier, inc=1, device_id=to, device_id_type=MESH)

    own = q % 2
    local_in[0].wait()
    own_rows = pl.ds(pl.multiple_of(own * ZR + x * SLOT + c * R, 16), R)

    @pl.when(handler)
    def _():
        wh[own_rows, :] = master_v[...].astype(BF16)

    @pl.when(jnp.logical_not(handler))
    def _():
        stage[...] = master_v[...].astype(BF16)

    pl.semaphore_wait(barrier, len(greeted))

    zcols, xcols = pl.ds(0, NZ), pl.ds(NZ, NX)

    def rows(zl, xx, half=0):
        return pl.multiple_of(zl * ZR + xx * SLOT + half * R, 16)

    def block(buf, zl, xx, cols, half=None):
        if half is None:
            return buf.at[pl.ds(rows(zl, xx), SLOT), cols]
        return buf.at[pl.ds(rows(zl, xx, half), R), cols]

    hcol = pl.multiple_of(c * H, 128)
    pcol = pl.multiple_of((1 - c) * H, 128)

    go(stage, wh.at[own_rows, :], part_s.at[0], part_r.at[0], partner, jnp.logical_not(handler))
    other_rows = pl.ds(pl.multiple_of(own * ZR + x * SLOT + (1 - c) * R, 16), R)

    go(residual.at[0, :, pl.ds(pcol, H)], resp, part_s.at[1], part_r.at[1], partner)
    go(cotangent.at[0], cot.at[pl.ds(T, T)], part_s.at[2], part_r.at[2], partner)

    first_sends = len(sends)

    def all_steps(owner, order):
        def slot_of(k):
            return (x, xl, xr, xo)[k]

        def towards(zl):
            goal = 2 * c + zl
            return jnp.logical_and(q >= goal, q < 3), jnp.logical_and(q <= goal, q > 0)

        def both(fixed, cond):
            return cond if fixed else False

        def own_in():
            got(wh.at[other_rows, :], part_r.at[0], owner)

        def turn(h):
            return c if h == 0 else 1 - c

        def ag_z_send(zl, h, cond):
            ref = block(wh, zl, x, zcols, turn(h))
            go_up, go_down = towards(zl)
            go(ref, ref, agz_s.at[zl, 0, h], agz_r.at[zl, h], up, both(cond, go_up))
            go(ref, ref, agz_s.at[zl, 1, h], agz_r.at[zl, h], down, both(cond, go_down))

        def ag_x_send(zl, h, cond):
            ref = block(wh, zl, x, zcols, turn(h))
            go(ref, ref, agx_s.at[zl, turn(h)], agx_r.at[zl, turn(h)], right, cond)
            go(ref, ref, agx_s.at[zl, 2 + turn(h)], agx_r.at[zl, 2 + turn(h)], left, cond)

        def ag_z(zl, h):
            cond = not (owner and zl is near)
            got(block(wh, zl, x, zcols, turn(h)), agz_r.at[zl, h], cond)
            ag_z_send(zl, h, cond)
            ag_x_send(zl, h, cond)

        def ag_left(zl):
            ref = block(wh, zl, xl, zcols, 0)
            got(ref, agx_r.at[zl, 0])
            go(ref, ref, agx_s.at[zl, 4], agx_r.at[zl, 4], right)

        def ag_right(zl):
            ref = block(wh, zl, xr, zcols, 1)
            got(ref, agx_r.at[zl, 3])
            go(ref, ref, agx_s.at[zl, 5], agx_r.at[zl, 5], left)

        def ag_end(zl):
            got(block(wh, zl, xl, zcols, 1), agx_r.at[zl, 1])
            got(block(wh, zl, xr, zcols, 0), agx_r.at[zl, 2])
            got(block(wh, zl, xo, zcols, 0), agx_r.at[zl, 4])
            got(block(wh, zl, xo, zcols, 1), agx_r.at[zl, 5])

        def ax_send(h):
            ref = block(wh, own, x, xcols, turn(h))
            go(ref, ref, axx_s.at[h], axx_r.at[h], right, owner)
            go(ref, ref, axx_s.at[2 + h], axx_r.at[2 + h], left, owner)

        def ax_left():
            ref = block(wh, own, xl, xcols, 0)
            got(ref, axx_r.at[c], owner)
            go(ref, ref, axx_s.at[4], axx_r.at[4], right, owner)

        def ax_right():
            ref = block(wh, own, xr, xcols, 1)
            got(ref, axx_r.at[3 - c], owner)
            go(ref, ref, axx_s.at[5], axx_r.at[5], left, owner)

        def ax_end():
            got(block(wh, own, xo, xcols, 0), axx_r.at[4], owner)
            got(block(wh, own, xo, xcols, 1), axx_r.at[5], owner)

        def ax_z_send(zl, k, cond):
            ref = block(wh, zl, slot_of(k), xcols)
            go_up, go_down = towards(zl)
            go(ref, ref, axz_s.at[zl, k, 0], axz_r.at[zl, k], up, both(cond, go_up))
            go(ref, ref, axz_s.at[zl, k, 1], axz_r.at[zl, k], down, both(cond, go_down))

        def ax_own(k):
            if k == 1:
                got(block(wh, own, xl, xcols, 1), axx_r.at[1 - c], owner)
            if k == 2:
                got(block(wh, own, xr, xcols, 0), axx_r.at[2 + c], owner)
            ax_z_send(near, k, owner)

        def ax_z(zl, k):
            cond = not (owner and zl is near)
            got(block(wh, zl, slot_of(k), xcols), axz_r.at[zl, k], cond)
            ax_z_send(zl, k, cond)

        def norm_rows(i, _):
            spot = pl.ds(pl.multiple_of(i * 16, 16), 16)
            raw = res[spot, :].astype(F32)
            scale = lax.rsqrt(jnp.mean(raw * raw, axis=1, keepdims=True) + norm_eps)
            inv[spot, :] = jnp.broadcast_to(scale, (16, 128))
            return 0

        def scales():
            local_in[3].wait()
            local_in[1].wait()
            lax.fori_loop(0, T // 16, norm_rows, 0)
            go(inv.at[pl.ds(0, T)], inv.at[pl.ds(T, T)], part_s.at[3], part_r.at[3], partner)

        def normed_rows(source, col, base):
            def run(i, _):
                spot = pl.ds(pl.multiple_of(i * 16, 16), 16)
                there = pl.ds(pl.multiple_of(base + i * 16, 16), 16)
                scale = inv[there, :][:, :1]
                factor = 1.0 + gain_v[:, pl.ds(hcol, H)]
                raw = source[spot, pl.ds(col, H)].astype(F32)
                normed[there, :] = (raw * scale * factor).astype(BF16)
                return 0

            lax.fori_loop(0, T // 16, run, 0)

        def normed_own():
            normed_rows(res, hcol, 0)

        def normed_other():
            got(inv.at[pl.ds(T, T)], part_r.at[3])
            got(resp, part_r.at[1])
            normed_rows(resp, 0, T)
            local_in[2].wait()
            got(cot.at[pl.ds(T, T)], part_r.at[2])

        def grad_rows(zl):
            def run(t, _):
                at = zl * ZR + t * TILE
                a = normed[:, pl.ds(pl.multiple_of(at, 128), TILE)]
                part = lax.dot_general(a, cot[...], (((0,), (0,)), ((), ())), preferred_element_type=F32)
                g[pl.ds(pl.multiple_of(at, 16), TILE), :] = (part * out_scale).astype(BF16)
                return 0

            lax.fori_loop(0, ZR // TILE, run, 0)

        def add_into(row, count, cols, terms, cond=True):
            step = 48

            def run(i, _):
                spot = pl.ds(pl.multiple_of(row + i * step, 16), step)
                here = pl.ds(pl.multiple_of(i * step, 16), step)
                total = g[spot, cols].astype(F32)
                for term in terms:
                    total = total + term[here, :].astype(F32)
                g[spot, cols] = total.astype(BF16)
                return 0

            when(cond, lambda: lax.fori_loop(0, count // step, run, 0))

        def rs_opp(zl):
            go(block(g, zl, xo, zcols, 0), opp.at[zl, 0], rsx_s.at[zl, 0], rsx_r.at[zl, 0], right)
            go(block(g, zl, xo, zcols, 1), opp.at[zl, 1], rsx_s.at[zl, 1], rsx_r.at[zl, 1], left)

        first_half, second_half = pl.ds(0, R), pl.ds(R, R)

        def rs_plain(zl):
            go(block(g, zl, xr, zcols, 1), full.at[zl, 0, second_half], rsx_s.at[zl, 4], rsx_r.at[zl, 4], right)
            go(block(g, zl, xl, zcols, 0), full.at[zl, 1, first_half], rsx_s.at[zl, 5], rsx_r.at[zl, 5], left)

        def rs_right(zl):
            got(opp.at[zl, 0], rsx_r.at[zl, 0])
            add_into(rows(zl, xr, 0), R, zcols, [opp.at[zl, 0]])
            go(block(g, zl, xr, zcols, 0), full.at[zl, 0, first_half], rsx_s.at[zl, 2], rsx_r.at[zl, 2], right)

        def rs_left(zl):
            got(opp.at[zl, 1], rsx_r.at[zl, 1])
            add_into(rows(zl, xl, 1), R, zcols, [opp.at[zl, 1]])
            go(block(g, zl, xl, zcols, 1), full.at[zl, 1, second_half], rsx_s.at[zl, 3], rsx_r.at[zl, 3], left)

        def rs_x(zl, h):
            part = (first_half, second_half)[h]
            got(full.at[zl, 0, part], rsx_r.at[zl, (2, 4)[h]])
            got(full.at[zl, 1, part], rsx_r.at[zl, (5, 3)[h]])
            add_into(rows(zl, x, h), R, zcols, [full.at[zl, 0, part], full.at[zl, 1, part]])

        def rs_z(zl, h):
            above, below = towards(zl)
            goal = 2 * c + zl
            high = zbuf.at[zl, 1, pl.ds(h * R, R)]
            low = zbuf.at[zl, 0, pl.ds(h * R, R)]
            got(high, rsz_r.at[zl, 1, h], above)
            add_into(rows(zl, x, h), R, zcols, [high], above)
            got(low, rsz_r.at[zl, 0, h], below)
            add_into(rows(zl, x, h), R, zcols, [low], below)
            ref = block(g, zl, x, zcols, h)
            go(ref, high, rsz_s.at[zl, 0, h], rsz_r.at[zl, 1, h], down, q > goal)
            go(ref, low, rsz_s.at[zl, 1, h], rsz_r.at[zl, 0, h], up, q < goal)

        def rx_z(zl, k):
            above, below = towards(zl)
            xx = slot_of(k)
            got(zxbuf.at[zl, 1, k], rxz_r.at[zl, 1, k], above)
            add_into(rows(zl, xx), SLOT, xcols, [zxbuf.at[zl, 1, k]], above)
            got(zxbuf.at[zl, 0, k], rxz_r.at[zl, 0, k], below)
            add_into(rows(zl, xx), SLOT, xcols, [zxbuf.at[zl, 0, k]], below)
            ref = block(g, zl, xx, xcols)
            goal = 2 * c + zl
            go(ref, zxbuf.at[zl, 1, k], rxz_s.at[zl, 0, k], rxz_r.at[zl, 1, k], down, q > goal)
            go(ref, zxbuf.at[zl, 0, k], rxz_s.at[zl, 1, k], rxz_r.at[zl, 0, k], up, q < goal)

        def rx_opp():
            go(block(g, own, xo, xcols, 0), oppx.at[0], rxx_s.at[0], rxx_r.at[0], right, owner)
            go(block(g, own, xo, xcols, 1), oppx.at[1], rxx_s.at[1], rxx_r.at[1], left, owner)

        def rx_plain():
            go(block(g, own, xr, xcols, 1), fullx.at[0, second_half], rxx_s.at[4], rxx_r.at[4], right, owner)
            go(block(g, own, xl, xcols, 0), fullx.at[1, first_half], rxx_s.at[5], rxx_r.at[5], left, owner)

        def rx_right():
            got(oppx.at[0], rxx_r.at[0], owner)
            add_into(rows(own, xr, 0), R, xcols, [oppx.at[0]], owner)
            go(block(g, own, xr, xcols, 0), fullx.at[0, first_half], rxx_s.at[2], rxx_r.at[2], right, owner)

        def rx_left():
            got(oppx.at[1], rxx_r.at[1], owner)
            add_into(rows(own, xl, 1), R, xcols, [oppx.at[1]], owner)
            go(block(g, own, xl, xcols, 1), fullx.at[1, second_half], rxx_s.at[3], rxx_r.at[3], left, owner)

        def rx_end():
            for h, part in ((0, first_half), (1, second_half)):
                got(fullx.at[0, part], rxx_r.at[(2, 4)[h]], owner)
                got(fullx.at[1, part], rxx_r.at[(5, 3)[h]], owner)
                add_into(rows(own, x, h), R, xcols, [fullx.at[0, part], fullx.at[1, part]], owner)

        grad_mine = [
            pltpu.make_async_copy(g.at[own_rows, cols], grad_o.at[:, cols], loc.at[10 + k])
            for k, cols in enumerate((zcols, xcols))
        ]

        def grad_out(k):
            cols = (zcols, xcols)[k]
            when(owner, lambda: grad_mine[k].start())
            go(g.at[other_rows, cols], grad_o.at[:, cols], part_s.at[8 + k], part_r.at[8 + k], partner, owner)

        def outer_start():
            local_in[4].wait()
            local_in[5].wait()
            for b in range(R // (FRAGS * FR_ROWS)):
                first = me * (R // FR_ROWS) + b * FRAGS
                spot = pl.ds(b * FR_ROWS, FR_ROWS)
                term = jnp.zeros((FR_ROWS, DV), F32)
                for k in range(FRAGS):
                    taken = (frag[first + k] == 0).astype(F32)
                    term = term + taken * anchor_v[pl.ds((b * FRAGS + k) * FR_ROWS, FR_ROWS), :]
                for k in range(HIST):
                    taken = (delay[0, b] == k + 1).astype(F32)
                    term = term - taken * hist_v[k, spot, :]
                oterm[spot, :] = term
            obuf[y] = oterm[:, pl.ds(pl.multiple_of(y * QUART, 128), QUART)]
            for k in range(1, 4):
                yy = (y + k) % 4
                go(
                    oterm.at[:, pl.ds(pl.multiple_of(yy * QUART, 128), QUART)], obuf.at[y],
                    oy_s.at[k], oy_r.at[k], {"replica": yy * 2 + zh},
                )

        def outer_mid():
            for k in range(1, 4):
                got(obuf.at[(y + 4 - k) % 4], oy_r.at[k])
            osum[...] = (obuf[0] + obuf[1]) + (obuf[2] + obuf[3])
            go(osum, ozh, oz_s, oz_r, {"replica": y * 2 + 1 - zh})

        def outer_last():
            got(ozh, oz_r)
            mine = pl.ds(pl.multiple_of(y * QUART, 128), QUART)
            od[:, mine] = (osum[...] + ozh[...]) * 0.125
            for k in range(1, 4):
                go(od.at[:, mine], od.at[:, mine], ob_s.at[k], ob_r.at[k], {"replica": ((y + k) % 4) * 2 + zh})

        def outer_out():
            for k in range(1, 4):
                theirs = pl.ds(pl.multiple_of(((y + 4 - k) % 4) * QUART, 128), QUART)
                got(od.at[:, theirs], ob_r.at[k])

        def near_far_values(zl, first):
            def run(n, _):
                cols = pl.ds(pl.multiple_of(n * 256, 128), 256)
                part = jnp.dot(
                    normed[:, pl.ds(pl.multiple_of(zl * ZR, 128), ZR)],
                    wh[pl.ds(pl.multiple_of(zl * ZR, 16), ZR), cols],
                    preferred_element_type=F32,
                )
                if first:
                    vacc[:, cols] = part
                else:
                    vacc[:, cols] = vacc[:, cols] + part
                return 0

            lax.fori_loop(0, DV // 256, run, 0)

        def dnormed(zl):
            def run(t, _):
                at = zl * ZR + t * TILE
                part = lax.dot_general(
                    cot[...], wh[pl.ds(pl.multiple_of(at, 16), TILE), :], (((1,), (1,)), ((), ())),
                    preferred_element_type=F32,
                )
                dn[:, pl.ds(pl.multiple_of(at, 128), TILE)] = part * out_scale
                return 0

            lax.fori_loop(0, ZR // TILE, run, 0)

        def sums(zl, first):
            at = pl.multiple_of(zl * ZR, 128)
            factor = 1.0 + gain_v[:, pl.ds(pl.multiple_of(hcol + at, 128), ZR)]

            def part_of(source, col, base, total):
                def run(i, total):
                    spot = pl.ds(pl.multiple_of(i * 16, 16), 16)
                    there = pl.ds(pl.multiple_of(base + i * 16, 16), 16)
                    unit = source[spot, pl.ds(col, ZR)].astype(F32) * inv[there, :][:, :1]
                    prod = dn[there, pl.ds(at, ZR)] * unit
                    scaled = prod * factor
                    lanes = scaled[:, :128]
                    for k in range(1, ZR // 128):
                        lanes = lanes + scaled[:, k * 128 : (k + 1) * 128]
                    if first:
                        rs[there, :] = lanes
                    else:
                        rs[there, :] = rs[there, :] + lanes
                    return total + (prod[:8] + prod[8:])

                return lax.fori_loop(0, T // 16, run, total)

            total = jnp.zeros((8, ZR), F32)
            total = part_of(res, pl.multiple_of(hcol + at, 128), 0, total)
            total = part_of(resp, at, T, total)
            ggt[:, pl.ds(at, ZR)] = jnp.sum(total, axis=0, keepdims=True)

        def input_grad(source, col, base):
            factor = 1.0 + gain_v[:, pl.ds(hcol, H)]

            def run(i, _):
                spot = pl.ds(pl.multiple_of(i * 16, 16), 16)
                there = pl.ds(pl.multiple_of(base + i * 16, 16), 16)
                scale = inv[there, :][:, :1]
                unit = source[spot, pl.ds(col, H)].astype(F32) * scale
                there_too = pl.ds(pl.multiple_of(T - base + i * 16, 16), 16)
                mean = jnp.sum(rs[there, :] + rsp[there_too, :], axis=1, keepdims=True) * (1.0 / D)
                ig[there, :] = (scale * (dn[there, :] * factor - unit * mean)).astype(BF16)
                return 0

            lax.fori_loop(0, T // 16, run, 0)

        delta_copy = pltpu.make_async_copy(od, delta_o, loc.at[6])
        ig_copy = pltpu.make_async_copy(ig.at[pl.ds(0, T)], igrad_o.at[0, :, pl.ds(hcol, H)], loc.at[7])
        values_copy = pltpu.make_async_copy(vout, values_o.at[0], loc.at[8])
        gain_copy = pltpu.make_async_copy(ggt, ggrad_o.at[:, pl.ds(hcol, H)], loc.at[9])

        def values_send():
            go(vacc.at[pl.ds(T, T)], vrecv, part_s.at[4], part_r.at[4], partner)

        def sums_send():
            go(rs, rsp, part_s.at[5], part_r.at[5], partner)
            ggx[x] = ggt[...]
            for k in range(1, 4):
                go(ggx.at[x], ggx.at[x], gx_s.at[k], gx_r.at[k], dev(q, (x + k) % 4, c))

        def igrad_other():
            got(rsp, part_r.at[5])
            input_grad(resp, 0, T)
            go(ig.at[pl.ds(T, T)], igrad_o.at[0, :, pl.ds(hcol, H)], part_s.at[6], part_r.at[6], partner)

        def igrad_own():
            input_grad(res, hcol, 0)
            ig_copy.start()

        def gain_x():
            for k in range(1, 4):
                got(ggx.at[(x + 4 - k) % 4], gx_r.at[k])
            ggz[q] = (ggx[0] + ggx[1]) + (ggx[2] + ggx[3])
            for k in range(1, 4):
                go(ggz.at[q], ggz.at[q], gz_s.at[k], gz_r.at[k], dev((q + k) % 4, x, c))

        def gain_z():
            for k in range(1, 4):
                got(ggz.at[(q + 4 - k) % 4], gz_r.at[k])
            ggt[...] = (ggz[0] + ggz[1]) + (ggz[2] + ggz[3])
            gain_copy.start()
            go(ggt, ggrad_o.at[:, pl.ds(hcol, H)], part_s.at[7], part_r.at[7], partner)

        def values_end():
            got(vrecv, part_r.at[4])
            vout[...] = ((vacc[pl.ds(0, T), :] + vrecv[...]) * out_scale).astype(BF16)
            values_copy.start()

        def delta_end():
            outer_out()
            delta_copy.start()

        steps = [
            own_in, lambda: ag_z_send(near, 0, owner), lambda: ag_z_send(near, 1, owner),
            lambda: ag_x_send(near, 0, owner), lambda: ag_x_send(near, 1, owner),
            lambda: ax_send(0), lambda: ax_send(1), ax_left, ax_right, ax_end,
            lambda: ax_own(0), lambda: ax_own(1), lambda: ax_own(2), lambda: ax_own(3),
            scales, normed_own, normed_other,
            rx_opp, rx_plain, rx_right, rx_left, rx_end, lambda: grad_out(0), lambda: grad_out(1),
            outer_start, outer_mid, outer_last, delta_end,
            values_send, sums_send, igrad_other, igrad_own, gain_x, gain_z, values_end,
        ]
        for zl, first in ((near, True), (far, False)):
            steps.append(lambda zl=zl: ag_z(zl, 0))
            steps.append(lambda zl=zl: ag_z(zl, 1))
            for run in (
                ag_left, ag_right, ag_end, grad_rows, rs_opp,
                rs_plain, rs_right, rs_left,
            ):
                steps.append(lambda run=run, zl=zl: run(zl))
            for run in (rs_x, rs_z):
                steps.append(lambda run=run, zl=zl: run(zl, 0))
                steps.append(lambda run=run, zl=zl: run(zl, 1))
            steps.append(lambda zl=zl: dnormed(zl))
            steps.append(lambda zl=zl, first=first: near_far_values(zl, first))
            steps.append(lambda zl=zl, first=first: sums(zl, first))
            for run in (ax_z, rx_z):
                for k in range(4):
                    steps.append(lambda run=run, zl=zl, k=k: run(zl, k))

        def finish():
            for k, cols in enumerate((zcols, xcols)):
                got(grad_o.at[:, cols], part_r.at[8 + k], not owner)
            got(igrad_o.at[0, :, pl.ds(pcol, H)], part_r.at[6])
            got(ggrad_o.at[:, pl.ds(pcol, H)], part_r.at[7])
            for item in grad_mine:
                when(owner, lambda item=item: item.wait())
            for item in (delta_copy, ig_copy, values_copy, gain_copy):
                item.wait()
            for cond, made in sends[first_sends:]:
                when(cond, lambda made=made: made.wait_send())

        for number in order:
            step(number, steps[number])
        step(-1, finish)
        del sends[first_sends:]

    for kind, order in enumerate(ORDERS):
        @pl.when(place == kind)
        def _(owner=kind < 2, order=order):
            all_steps(owner, order)

    for cond, made in sends:
        when(cond, lambda made=made: made.wait_send())


def main_call(frag, delay, residual, cotangent, gain, master, anchor, history):
    any_space = pl.BlockSpec(memory_space=pl.ANY)
    smem = pl.BlockSpec(memory_space=pltpu.SMEM)
    vm = pltpu.VMEM
    dma = pltpu.SemaphoreType.DMA
    nx = max(NX, 128)
    scratch = [
        vm((T, D), BF16), vm((T, H), BF16), vm((2 * T, DV), BF16), vm((1, D), F32),
        vm((R, DV), F32), vm((R, DV), F32), vm((HIST, PART, DV), F32),
        vm((H, DV), BF16), vm((R, DV), BF16), vm((H, DV), BF16), vm((2 * T, H), BF16),
        vm((2 * T, 128), F32), vm((2 * T, H), F32), vm((2 * T, DV), F32), vm((T, DV), F32),
        vm((T, DV), BF16), vm((2 * T, 128), F32), vm((2 * T, 128), F32), vm((2 * T, H), BF16),
        vm((4, 1, H), F32), vm((4, 1, H), F32), vm((1, H), F32),
        vm((2, 2, R, NZ), BF16), vm((2, 2, SLOT, NZ), BF16), vm((2, 2, SLOT, NZ), BF16),
        vm((2, 2, 4, SLOT, nx), BF16), vm((2, R, nx), BF16), vm((2, SLOT, nx), BF16),
        vm((PART, DV), F32), vm((4, PART, QUART), F32), vm((PART, QUART), F32),
        vm((PART, QUART), F32), vm((PART, DV), F32),
        dma((12,)), dma((10,)), dma((10,)), dma((2, 2, 2)), dma((2, 2)), dma((2, 6)), dma((2, 6)),
        dma((6,)), dma((6,)), dma((2, 4, 2)), dma((2, 4)),
        dma((2, 6)), dma((2, 6)), dma((2, 2, 2)), dma((2, 2, 2)),
        dma((2, 2, 4)), dma((2, 2, 4)), dma((6,)), dma((6,)),
        dma((4,)), dma((4,)), dma((4,)), dma((4,)),
        dma((4,)), dma((4,)), dma, dma, dma((4,)), dma((4,)),
    ]
    return pl.pallas_call(
        main_kernel,
        out_shape=(
            jax.ShapeDtypeStruct((1, T, DV), BF16),
            jax.ShapeDtypeStruct((1, T, D), BF16),
            jax.ShapeDtypeStruct((1, D), F32),
            jax.ShapeDtypeStruct((R, DV), BF16),
            jax.ShapeDtypeStruct((PART, DV), F32),
        ),
        in_specs=[smem, smem] + [any_space] * 6,
        out_specs=(any_space,) * 5,
        scratch_shapes=scratch,
        compiler_params=pltpu.CompilerParams(
            collective_id=0, has_side_effects=True, vmem_limit_bytes=44 * 1024 * 1024
        ),
        name="inner_step",
    )(frag, delay, residual, cotangent, gain, master, anchor, history)


def update_kernel(
    frag, grad, delta, master, first, second, anchor, momentum, values, igrad, ggrad,
    master_o, first_o, second_o, anchor_o, momentum_o, values_o, igrad_o, ggrad_o,
    grad_v, delta_v, master_v, first_v, second_v, anchor_v, momentum_v,
    master_n, first_n, second_n, load, load_small, stored, through,
):
    rows = FRAGS * FR_ROWS
    groups = R // rows
    spots = [pl.ds(i * rows, rows) for i in range(groups)]
    small = [
        pltpu.make_async_copy(grad, grad_v, load_small.at[0]),
        pltpu.make_async_copy(delta, delta_v, load_small.at[1]),
    ]
    for item in small:
        item.start()
    loads = []
    for i, at in enumerate(spots):
        loads.append([
            pltpu.make_async_copy(src, dst, load.at[i, k])
            for k, (src, dst) in enumerate((
                (master.at[0, at], master_v.at[at]),
                (first.at[0, at], first_v.at[at]),
                (second.at[0, at], second_v.at[at]),
                (anchor.at[at], anchor_v.at[at]),
                (momentum.at[at], momentum_v.at[at]),
            ))
        ])
    for item in loads[0] + loads[1] + loads[2]:
        item.start()
    passed = [
        pltpu.make_async_copy(src, dst, through.at[k])
        for k, (src, dst) in enumerate(((igrad, igrad_o), (values, values_o), (ggrad, ggrad_o)))
    ]
    for item in passed:
        item.start()
    for item in small:
        item.wait()
    begin = lax.axis_index("fsdp") * (R // FR_ROWS)
    stores = []
    for i, at in enumerate(spots):
        for item in loads[i]:
            item.wait()
        chosen = jnp.int32(0)
        for k in range(1, FRAGS):
            chosen = chosen + jnp.where(frag[begin + i * FRAGS + k] == 0, k, 0)
        block = pl.ds(pl.multiple_of(i * rows + chosen * FR_ROWS, FR_ROWS), FR_ROWS)

        change = delta_v[pl.ds(i * FR_ROWS, FR_ROWS), :]
        anchor_old = anchor_v[block, :]
        momentum_part = outer_beta * momentum_v[block, :] + change
        anchor_part = anchor_old - outer_rate * (change + outer_beta * momentum_part)
        anchor_v[block, :] = anchor_part
        momentum_v[block, :] = momentum_part

        def store(k, src, dst):
            item = pltpu.make_async_copy(src, dst, stored.at[i, k])
            item.start()
            stores.append(item)

        store(0, anchor_v.at[at], anchor_o.at[at])
        store(1, momentum_v.at[at], momentum_o.at[at])
        for piece in range(rows // 16):
            part = pl.ds(i * rows + piece * 16, 16)
            gradient = grad_v[part, :].astype(F32)
            weights = master_v[part, :]
            first_new = beta_one * first_v[part, :] + (1.0 - beta_one) * gradient
            second_new = beta_two * second_v[part, :] + (1.0 - beta_two) * gradient * gradient
            first_n[part, :] = first_new
            second_n[part, :] = second_new
            master_n[part, :] = weights - inner_rate * (
                first_new / (jnp.sqrt(second_new) + adam_eps) + weight_decay * weights
            )
        store(2, first_n.at[at], first_o.at[0, at])
        store(3, second_n.at[at], second_o.at[0, at])
        master_n[block, :] = mix_weight * master_n[block, :] + (1.0 - mix_weight) * anchor_part
        store(4, master_n.at[at], master_o.at[0, at])
    for item in stores + passed:
        item.wait()


def update_call(frag, grad, delta, master, first, second, anchor, momentum, values, igrad, ggrad):
    any_space = pl.BlockSpec(memory_space=pl.ANY)
    like3 = jax.ShapeDtypeStruct((1, R, DV), F32)
    like2 = jax.ShapeDtypeStruct((R, DV), F32)
    dma = pltpu.SemaphoreType.DMA
    whole = pltpu.VMEM((R, DV), F32)
    groups = R // (FRAGS * FR_ROWS)
    return pl.pallas_call(
        update_kernel,
        out_shape=(
            like3, like3, like3, like2, like2,
            jax.ShapeDtypeStruct((1, T, DV), BF16),
            jax.ShapeDtypeStruct((1, T, D), BF16),
            jax.ShapeDtypeStruct((1, D), F32),
        ),
        in_specs=[pl.BlockSpec(memory_space=pltpu.SMEM)] + [any_space] * 10,
        out_specs=(any_space,) * 8,
        scratch_shapes=[pltpu.VMEM((R, DV), BF16), pltpu.VMEM((PART, DV), F32)]
        + [whole] * 8
        + [dma((groups, 5)), dma((2,)), dma((groups, 5)), dma((3,))],
        compiler_params=pltpu.CompilerParams(vmem_limit_bytes=16 * 1024 * 1024),
        name="update",
    )(frag, grad, delta, master, first, second, anchor, momentum, values, igrad, ggrad)


def body(
    residual, cotangent, norm_gain, master, first_moment, second_moment,
    anchor, outer_momentum, history, fragment, delay,
):
    (
        residual, cotangent, norm_gain, master, first_moment, second_moment,
        anchor, outer_momentum, history, fragment, delay,
    ) = [
        pltpu.with_memory_space_constraint(item, pltpu.HBM)
        for item in (
            residual, cotangent, norm_gain, master, first_moment, second_moment,
            anchor, outer_momentum, history, fragment, delay,
        )
    ]
    values, input_grad, gain_grad, gradient, delta = main_call(
        fragment, delay, residual, cotangent, norm_gain, master, anchor, history
    )
    new_master, new_first, new_second, new_anchor, new_momentum, values, input_grad, gain_grad = update_call(
        fragment, gradient, delta, master, first_moment, second_moment, anchor, outer_momentum,
        values, input_grad, gain_grad,
    )
    return (
        values, input_grad, gain_grad, new_master, new_first, new_second, new_anchor, new_momentum,
    )


def solution(mesh):
    rows = P("replica", "fsdp", None)
    both = P("fsdp", None)
    return jax.shard_map(
        body,
        mesh=mesh,
        in_specs=(
            rows, rows, P("replica", None), rows, rows, rows, both, both,
            P("replica", None, "fsdp", None), P(), P("replica", "fsdp"),
        ),
        out_specs=(rows, rows, P("replica", None), rows, rows, rows, both, both),
        check_vma=False,
    )
```

```python
import jax
import jax.numpy as jnp
from jax import lax
from jax.experimental import pallas as pl
from jax.experimental.pallas import tpu as pltpu
from jax.sharding import PartitionSpec as P

D = 4608
DV = 1024
FRAGS = 6
FR_ROWS = 8
HIST = 4

T = 256
R = 144
SLOT = 2 * R
ZR = 4 * SLOT
H = 2 * ZR
TILE = 384
NZ = 640
NX = DV - NZ
PART = R // FRAGS
QUART = DV // 4

norm_eps = 1e-06
beta_one = 0.9
beta_two = 0.95
inner_rate = 0.01
weight_decay = 0.1
adam_eps = 1e-08
outer_beta = 0.9
outer_rate = 0.7
mix_weight = 0.5
out_scale = float(D) ** (-0.5)

MESH = pl.DeviceIdType.MESH
F32 = jnp.float32
BF16 = jnp.bfloat16


ORDERS = [
    [
        1, 5, 0, 10, 6, 4, 14, 3, 2, 60, 8, 12, 7, 11, 61, 37, 38, 9, 78, 13, 16, 39, 15, 77, 79, 24, 62, 63,
        50, 49, 80, 65, 64, 40, 51, 82, 25, 84, 66, 74, 81, 68, 41, 83, 26, 67, 76, 69, 75, 29, 42, 27, 44,
        70, 56, 43, 57, 71, 32, 73, 72, 58, 59, 17, 30, 28, 18, 19, 20, 46, 31, 33, 48, 34, 45, 47, 22, 21,
        23,
    ],
    [
        1, 5, 24, 0, 6, 2, 10, 4, 60, 8, 7, 11, 3, 14, 12, 61, 16, 78, 15, 37, 38, 9, 25, 13, 77, 79, 40, 39,
        65, 50, 62, 63, 80, 49, 64, 74, 66, 67, 51, 83, 75, 81, 69, 82, 68, 41, 76, 28, 26, 29, 84, 56, 57,
        42, 58, 30, 59, 17, 71, 70, 44, 43, 18, 73, 32, 31, 72, 20, 19, 27, 34, 45, 46, 47, 48, 33, 22, 21,
        23,
    ],
    [
        14, 35, 15, 16, 36, 65, 60, 53, 40, 54, 67, 61, 37, 52, 66, 38, 55, 83, 78, 63, 69, 77, 41, 81, 62,
        39, 24, 58, 68, 79, 82, 57, 49, 42, 80, 51, 84, 50, 43, 44, 56, 25, 71, 59, 64, 73, 74, 76, 45, 70,
        26, 29, 46, 75, 72, 47, 28, 30, 48, 32, 33, 27, 34, 31,
    ],
    [
        14, 15, 16, 40, 41, 65, 66, 83, 84, 24, 35, 25, 57, 43, 69, 81, 36, 58, 82, 67, 68, 53, 56, 38, 54,
        60, 37, 59, 61, 71, 26, 73, 44, 55, 39, 52, 27, 42, 63, 49, 62, 70, 77, 51, 50, 46, 72, 45, 64, 47,
        79, 48, 78, 80, 74, 76, 29, 75, 30, 32, 31, 28, 33, 34,
    ],
]


def step(number, run):
    run()


def main_kernel(
    frag, delay, residual, cotangent, gain, master, anchor, history,
    values_o, igrad_o, ggrad_o, grad_o, delta_o,
    res, resp, cot, gain_v, master_v, anchor_v, hist_v,
    wh, stage, g, normed, inv, dn, vacc, vrecv, vout, rs, rsp, ig, ggx, ggz, ggt,
    opp, full, zbuf, zxbuf, oppx, fullx, oterm, obuf, osum, ozh, od,
    loc, part_s, part_r, agz_s, agz_r, agx_s, agx_r, axx_s, axx_r, axz_s, axz_r,
    rsx_s, rsx_r, rsz_s, rsz_r, rxz_s, rxz_r, rxx_s, rxx_r, gx_s, gx_r, gz_s, gz_r,
    oy_s, oy_r, oz_s, oz_r, ob_s, ob_r, ready_y, ready_z,
):
    me = lax.axis_index("fsdp")
    rep = lax.axis_index("replica")
    q, x, c = me // 8, (me // 2) % 4, me % 2
    y, zh = rep // 2, rep % 2
    xr, xl, xo = (x + 1) % 4, (x + 3) % 4, (x + 2) % 4
    handler = c == q // 2
    place = jnp.where(c == 0, q, 3 - q)
    near = jnp.where(place == 0, c, 1 - c)
    far = 1 - near

    def dev(qq, xx, cc):
        return {"fsdp": qq * 8 + xx * 2 + cc}

    partner, right, left = dev(q, x, 1 - c), dev(q, xr, c), dev(q, xl, c)
    up, down = dev(q + 1, x, c), dev(q - 1, x, c)

    sends = []

    def copy(src, dst, send, recv, to):
        return pltpu.make_async_remote_copy(
            src_ref=src, dst_ref=dst, send_sem=send, recv_sem=recv, device_id=to, device_id_type=MESH
        )

    def when(cond, run):
        if cond is True:
            run()
        elif cond is not False:
            @pl.when(cond)
            def _():
                run()

    def go(src, dst, send, recv, to, cond=True):
        made = copy(src, dst, send, recv, to)
        when(cond, lambda: made.start())
        sends.append((cond, made))

    def got(dst, recv, cond=True):
        made = copy(dst, dst, part_s.at[0], recv, partner)
        when(cond, lambda: made.wait_recv())

    local_in = [
        pltpu.make_async_copy(master.at[0], master_v, loc.at[0]),
        pltpu.make_async_copy(residual.at[0], res, loc.at[1]),
        pltpu.make_async_copy(cotangent.at[0], cot.at[pl.ds(0, T)], loc.at[2]),
        pltpu.make_async_copy(gain, gain_v, loc.at[3]),
        pltpu.make_async_copy(anchor, anchor_v, loc.at[4]),
        pltpu.make_async_copy(history.at[0], hist_v, loc.at[5]),
    ]
    for item in local_in:
        item.start()

    barrier = pltpu.get_barrier_semaphore()
    greeted = [partner]
    greeted += [dev(q, (x + k) % 4, c) for k in range(1, 4)]
    greeted += [dev((q + k) % 4, x, c) for k in range(1, 4)]
    for to in greeted:
        pl.semaphore_signal(barrier, inc=1, device_id=to, device_id_type=MESH)

    other_z = {"replica": y * 2 + 1 - zh}

    @pl.when(zh == 0)
    def _():
        pl.semaphore_signal(barrier, inc=1, device_id=other_z, device_id_type=MESH)

    for k in range(1, 4):
        @pl.when(y + k < 4)
        def _(k=k):
            pl.semaphore_signal(
                barrier, inc=1, device_id={"replica": (y + k) * 2 + zh}, device_id_type=MESH
            )

    own = q % 2
    local_in[0].wait()
    own_rows = pl.ds(pl.multiple_of(own * ZR + x * SLOT + c * R, 16), R)

    @pl.when(handler)
    def _():
        wh[own_rows, :] = master_v[...].astype(BF16)

    @pl.when(jnp.logical_not(handler))
    def _():
        stage[...] = master_v[...].astype(BF16)

    pl.semaphore_wait(barrier, len(greeted) + y + zh)

    @pl.when(zh == 1)
    def _():
        pl.semaphore_signal(ready_z, inc=1, device_id=other_z, device_id_type=MESH)

    for k in range(1, 4):
        @pl.when(y >= k)
        def _(k=k):
            pl.semaphore_signal(
                ready_y, inc=1, device_id={"replica": (y - k) * 2 + zh}, device_id_type=MESH
            )

    zcols, xcols = pl.ds(0, NZ), pl.ds(NZ, NX)

    def rows(zl, xx, half=0):
        return pl.multiple_of(zl * ZR + xx * SLOT + half * R, 16)

    def block(buf, zl, xx, cols, half=None):
        if half is None:
            return buf.at[pl.ds(rows(zl, xx), SLOT), cols]
        return buf.at[pl.ds(rows(zl, xx, half), R), cols]

    hcol = pl.multiple_of(c * H, 128)
    pcol = pl.multiple_of((1 - c) * H, 128)

    go(stage, wh.at[own_rows, :], part_s.at[0], part_r.at[0], partner, jnp.logical_not(handler))
    other_rows = pl.ds(pl.multiple_of(own * ZR + x * SLOT + (1 - c) * R, 16), R)

    go(residual.at[0, :, pl.ds(pcol, H)], resp, part_s.at[1], part_r.at[1], partner)
    go(cotangent.at[0], cot.at[pl.ds(T, T)], part_s.at[2], part_r.at[2], partner)

    first_sends = len(sends)

    def all_steps(owner, order):
        def slot_of(k):
            return (x, xl, xr, xo)[k]

        def towards(zl):
            goal = 2 * c + zl
            return jnp.logical_and(q >= goal, q < 3), jnp.logical_and(q <= goal, q > 0)

        def both(fixed, cond):
            return cond if fixed else False

        def own_in():
            got(wh.at[other_rows, :], part_r.at[0], owner)

        def turn(h):
            return c if h == 0 else 1 - c

        def ag_z_send(zl, h, cond):
            ref = block(wh, zl, x, zcols, turn(h))
            go_up, go_down = towards(zl)
            go(ref, ref, agz_s.at[zl, 0, h], agz_r.at[zl, h], up, both(cond, go_up))
            go(ref, ref, agz_s.at[zl, 1, h], agz_r.at[zl, h], down, both(cond, go_down))

        def ag_x_send(zl, h, cond):
            ref = block(wh, zl, x, zcols, turn(h))
            go(ref, ref, agx_s.at[zl, turn(h)], agx_r.at[zl, turn(h)], right, cond)
            go(ref, ref, agx_s.at[zl, 2 + turn(h)], agx_r.at[zl, 2 + turn(h)], left, cond)

        def ag_z(zl, h):
            cond = not (owner and zl is near)
            got(block(wh, zl, x, zcols, turn(h)), agz_r.at[zl, h], cond)
            ag_z_send(zl, h, cond)
            ag_x_send(zl, h, cond)

        def ag_left(zl):
            ref = block(wh, zl, xl, zcols, 0)
            got(ref, agx_r.at[zl, 0])
            go(ref, ref, agx_s.at[zl, 4], agx_r.at[zl, 4], right)

        def ag_right(zl):
            ref = block(wh, zl, xr, zcols, 1)
            got(ref, agx_r.at[zl, 3])
            go(ref, ref, agx_s.at[zl, 5], agx_r.at[zl, 5], left)

        def ag_end(zl):
            got(block(wh, zl, xl, zcols, 1), agx_r.at[zl, 1])
            got(block(wh, zl, xr, zcols, 0), agx_r.at[zl, 2])
            got(block(wh, zl, xo, zcols, 0), agx_r.at[zl, 4])
            got(block(wh, zl, xo, zcols, 1), agx_r.at[zl, 5])

        def ax_send(h):
            ref = block(wh, own, x, xcols, turn(h))
            go(ref, ref, axx_s.at[h], axx_r.at[h], right, owner)
            go(ref, ref, axx_s.at[2 + h], axx_r.at[2 + h], left, owner)

        def ax_left():
            ref = block(wh, own, xl, xcols, 0)
            got(ref, axx_r.at[c], owner)
            go(ref, ref, axx_s.at[4], axx_r.at[4], right, owner)

        def ax_right():
            ref = block(wh, own, xr, xcols, 1)
            got(ref, axx_r.at[3 - c], owner)
            go(ref, ref, axx_s.at[5], axx_r.at[5], left, owner)

        def ax_end():
            got(block(wh, own, xo, xcols, 0), axx_r.at[4], owner)
            got(block(wh, own, xo, xcols, 1), axx_r.at[5], owner)

        def ax_z_send(zl, k, cond):
            ref = block(wh, zl, slot_of(k), xcols)
            go_up, go_down = towards(zl)
            go(ref, ref, axz_s.at[zl, k, 0], axz_r.at[zl, k], up, both(cond, go_up))
            go(ref, ref, axz_s.at[zl, k, 1], axz_r.at[zl, k], down, both(cond, go_down))

        def ax_own(k):
            if k == 1:
                got(block(wh, own, xl, xcols, 1), axx_r.at[1 - c], owner)
            if k == 2:
                got(block(wh, own, xr, xcols, 0), axx_r.at[2 + c], owner)
            ax_z_send(near, k, owner)

        def ax_z(zl, k):
            cond = not (owner and zl is near)
            got(block(wh, zl, slot_of(k), xcols), axz_r.at[zl, k], cond)
            ax_z_send(zl, k, cond)

        def norm_rows(i, _):
            spot = pl.ds(pl.multiple_of(i * 16, 16), 16)
            raw = res[spot, :].astype(F32)
            scale = lax.rsqrt(jnp.mean(raw * raw, axis=1, keepdims=True) + norm_eps)
            inv[spot, :] = jnp.broadcast_to(scale, (16, 128))
            return 0

        def scales():
            local_in[3].wait()
            local_in[1].wait()
            lax.fori_loop(0, T // 16, norm_rows, 0)
            go(inv.at[pl.ds(0, T)], inv.at[pl.ds(T, T)], part_s.at[3], part_r.at[3], partner)

        def normed_rows(source, col, base):
            def run(i, _):
                spot = pl.ds(pl.multiple_of(i * 16, 16), 16)
                there = pl.ds(pl.multiple_of(base + i * 16, 16), 16)
                scale = inv[there, :][:, :1]
                factor = 1.0 + gain_v[:, pl.ds(hcol, H)]
                raw = source[spot, pl.ds(col, H)].astype(F32)
                normed[there, :] = (raw * scale * factor).astype(BF16)
                return 0

            lax.fori_loop(0, T // 16, run, 0)

        def normed_own():
            normed_rows(res, hcol, 0)

        def normed_other():
            got(inv.at[pl.ds(T, T)], part_r.at[3])
            got(resp, part_r.at[1])
            normed_rows(resp, 0, T)
            local_in[2].wait()
            got(cot.at[pl.ds(T, T)], part_r.at[2])

        def grad_rows(zl):
            def run(t, _):
                at = zl * ZR + t * TILE
                a = normed[:, pl.ds(pl.multiple_of(at, 128), TILE)]
                part = lax.dot_general(a, cot[...], (((0,), (0,)), ((), ())), preferred_element_type=F32)
                g[pl.ds(pl.multiple_of(at, 16), TILE), :] = (part * out_scale).astype(BF16)
                return 0

            lax.fori_loop(0, ZR // TILE, run, 0)

        def add_into(row, count, cols, terms, cond=True):
            step = 48

            def run(i, _):
                spot = pl.ds(pl.multiple_of(row + i * step, 16), step)
                here = pl.ds(pl.multiple_of(i * step, 16), step)
                total = g[spot, cols].astype(F32)
                for term in terms:
                    total = total + term[here, :].astype(F32)
                g[spot, cols] = total.astype(BF16)
                return 0

            when(cond, lambda: lax.fori_loop(0, count // step, run, 0))

        def rs_opp(zl):
            go(block(g, zl, xo, zcols, 0), opp.at[zl, 0], rsx_s.at[zl, 0], rsx_r.at[zl, 0], right)
            go(block(g, zl, xo, zcols, 1), opp.at[zl, 1], rsx_s.at[zl, 1], rsx_r.at[zl, 1], left)

        first_half, second_half = pl.ds(0, R), pl.ds(R, R)

        def rs_plain(zl):
            go(block(g, zl, xr, zcols, 1), full.at[zl, 0, second_half], rsx_s.at[zl, 4], rsx_r.at[zl, 4], right)
            go(block(g, zl, xl, zcols, 0), full.at[zl, 1, first_half], rsx_s.at[zl, 5], rsx_r.at[zl, 5], left)

        def rs_right(zl):
            got(opp.at[zl, 0], rsx_r.at[zl, 0])
            add_into(rows(zl, xr, 0), R, zcols, [opp.at[zl, 0]])
            go(block(g, zl, xr, zcols, 0), full.at[zl, 0, first_half], rsx_s.at[zl, 2], rsx_r.at[zl, 2], right)

        def rs_left(zl):
            got(opp.at[zl, 1], rsx_r.at[zl, 1])
            add_into(rows(zl, xl, 1), R, zcols, [opp.at[zl, 1]])
            go(block(g, zl, xl, zcols, 1), full.at[zl, 1, second_half], rsx_s.at[zl, 3], rsx_r.at[zl, 3], left)

        def rs_x(zl, h):
            part = (first_half, second_half)[h]
            got(full.at[zl, 0, part], rsx_r.at[zl, (2, 4)[h]])
            got(full.at[zl, 1, part], rsx_r.at[zl, (5, 3)[h]])
            add_into(rows(zl, x, h), R, zcols, [full.at[zl, 0, part], full.at[zl, 1, part]])

        def rs_z(zl, h):
            above, below = towards(zl)
            goal = 2 * c + zl
            high = zbuf.at[zl, 1, pl.ds(h * R, R)]
            low = zbuf.at[zl, 0, pl.ds(h * R, R)]
            got(high, rsz_r.at[zl, 1, h], above)
            add_into(rows(zl, x, h), R, zcols, [high], above)
            got(low, rsz_r.at[zl, 0, h], below)
            add_into(rows(zl, x, h), R, zcols, [low], below)
            ref = block(g, zl, x, zcols, h)
            go(ref, high, rsz_s.at[zl, 0, h], rsz_r.at[zl, 1, h], down, q > goal)
            go(ref, low, rsz_s.at[zl, 1, h], rsz_r.at[zl, 0, h], up, q < goal)

        def rx_z(zl, k):
            above, below = towards(zl)
            xx = slot_of(k)
            got(zxbuf.at[zl, 1, k], rxz_r.at[zl, 1, k], above)
            add_into(rows(zl, xx), SLOT, xcols, [zxbuf.at[zl, 1, k]], above)
            got(zxbuf.at[zl, 0, k], rxz_r.at[zl, 0, k], below)
            add_into(rows(zl, xx), SLOT, xcols, [zxbuf.at[zl, 0, k]], below)
            ref = block(g, zl, xx, xcols)
            goal = 2 * c + zl
            go(ref, zxbuf.at[zl, 1, k], rxz_s.at[zl, 0, k], rxz_r.at[zl, 1, k], down, q > goal)
            go(ref, zxbuf.at[zl, 0, k], rxz_s.at[zl, 1, k], rxz_r.at[zl, 0, k], up, q < goal)

        def rx_opp():
            go(block(g, own, xo, xcols, 0), oppx.at[0], rxx_s.at[0], rxx_r.at[0], right, owner)
            go(block(g, own, xo, xcols, 1), oppx.at[1], rxx_s.at[1], rxx_r.at[1], left, owner)

        def rx_plain():
            go(block(g, own, xr, xcols, 1), fullx.at[0, second_half], rxx_s.at[4], rxx_r.at[4], right, owner)
            go(block(g, own, xl, xcols, 0), fullx.at[1, first_half], rxx_s.at[5], rxx_r.at[5], left, owner)

        def rx_right():
            got(oppx.at[0], rxx_r.at[0], owner)
            add_into(rows(own, xr, 0), R, xcols, [oppx.at[0]], owner)
            go(block(g, own, xr, xcols, 0), fullx.at[0, first_half], rxx_s.at[2], rxx_r.at[2], right, owner)

        def rx_left():
            got(oppx.at[1], rxx_r.at[1], owner)
            add_into(rows(own, xl, 1), R, xcols, [oppx.at[1]], owner)
            go(block(g, own, xl, xcols, 1), fullx.at[1, second_half], rxx_s.at[3], rxx_r.at[3], left, owner)

        def rx_end():
            for h, part in ((0, first_half), (1, second_half)):
                got(fullx.at[0, part], rxx_r.at[(2, 4)[h]], owner)
                got(fullx.at[1, part], rxx_r.at[(5, 3)[h]], owner)
                add_into(rows(own, x, h), R, xcols, [fullx.at[0, part], fullx.at[1, part]], owner)

        grad_mine = [
            pltpu.make_async_copy(g.at[own_rows, cols], grad_o.at[:, cols], loc.at[10 + k])
            for k, cols in enumerate((zcols, xcols))
        ]

        def grad_out(k):
            cols = (zcols, xcols)[k]
            when(owner, lambda: grad_mine[k].start())
            go(g.at[other_rows, cols], grad_o.at[:, cols], part_s.at[8 + k], part_r.at[8 + k], partner, owner)

        def outer_start():
            local_in[4].wait()
            local_in[5].wait()
            for b in range(R // (FRAGS * FR_ROWS)):
                first = me * (R // FR_ROWS) + b * FRAGS
                spot = pl.ds(b * FR_ROWS, FR_ROWS)
                term = jnp.zeros((FR_ROWS, DV), F32)
                for k in range(FRAGS):
                    taken = (frag[first + k] == 0).astype(F32)
                    term = term + taken * anchor_v[pl.ds((b * FRAGS + k) * FR_ROWS, FR_ROWS), :]
                for k in range(HIST):
                    taken = (delay[0, b] == k + 1).astype(F32)
                    term = term - taken * hist_v[k, spot, :]
                oterm[spot, :] = term
            @pl.when(y < 3)
            def _():
                pl.semaphore_wait(ready_y, 3 - y)

            obuf[y] = oterm[:, pl.ds(pl.multiple_of(y * QUART, 128), QUART)]
            for k in range(1, 4):
                yy = (y + k) % 4
                go(
                    oterm.at[:, pl.ds(pl.multiple_of(yy * QUART, 128), QUART)], obuf.at[y],
                    oy_s.at[k], oy_r.at[k], {"replica": yy * 2 + zh},
                )

        def outer_mid():
            for k in range(1, 4):
                got(obuf.at[(y + 4 - k) % 4], oy_r.at[k])
            osum[...] = (obuf[0] + obuf[1]) + (obuf[2] + obuf[3])
            @pl.when(zh == 0)
            def _():
                pl.semaphore_wait(ready_z, 1)

            go(osum, ozh, oz_s, oz_r, other_z)

        def outer_last():
            got(ozh, oz_r)
            mine = pl.ds(pl.multiple_of(y * QUART, 128), QUART)
            od[:, mine] = (osum[...] + ozh[...]) * 0.125
            for k in range(1, 4):
                go(od.at[:, mine], od.at[:, mine], ob_s.at[k], ob_r.at[k], {"replica": ((y + k) % 4) * 2 + zh})

        def outer_out():
            for k in range(1, 4):
                theirs = pl.ds(pl.multiple_of(((y + 4 - k) % 4) * QUART, 128), QUART)
                got(od.at[:, theirs], ob_r.at[k])

        def near_far_values(zl, first):
            def run(n, _):
                cols = pl.ds(pl.multiple_of(n * 256, 128), 256)
                part = jnp.dot(
                    normed[:, pl.ds(pl.multiple_of(zl * ZR, 128), ZR)],
                    wh[pl.ds(pl.multiple_of(zl * ZR, 16), ZR), cols],
                    preferred_element_type=F32,
                )
                if first:
                    vacc[:, cols] = part
                else:
                    vacc[:, cols] = vacc[:, cols] + part
                return 0

            lax.fori_loop(0, DV // 256, run, 0)

        def dnormed(zl):
            def run(t, _):
                at = zl * ZR + t * TILE
                part = lax.dot_general(
                    cot[...], wh[pl.ds(pl.multiple_of(at, 16), TILE), :], (((1,), (1,)), ((), ())),
                    preferred_element_type=F32,
                )
                dn[:, pl.ds(pl.multiple_of(at, 128), TILE)] = part * out_scale
                return 0

            lax.fori_loop(0, ZR // TILE, run, 0)

        def sums(zl, first):
            at = pl.multiple_of(zl * ZR, 128)
            factor = 1.0 + gain_v[:, pl.ds(pl.multiple_of(hcol + at, 128), ZR)]

            def part_of(source, col, base, total):
                def run(i, total):
                    spot = pl.ds(pl.multiple_of(i * 16, 16), 16)
                    there = pl.ds(pl.multiple_of(base + i * 16, 16), 16)
                    unit = source[spot, pl.ds(col, ZR)].astype(F32) * inv[there, :][:, :1]
                    prod = dn[there, pl.ds(at, ZR)] * unit
                    scaled = prod * factor
                    lanes = scaled[:, :128]
                    for k in range(1, ZR // 128):
                        lanes = lanes + scaled[:, k * 128 : (k + 1) * 128]
                    if first:
                        rs[there, :] = lanes
                    else:
                        rs[there, :] = rs[there, :] + lanes
                    return total + (prod[:8] + prod[8:])

                return lax.fori_loop(0, T // 16, run, total)

            total = jnp.zeros((8, ZR), F32)
            total = part_of(res, pl.multiple_of(hcol + at, 128), 0, total)
            total = part_of(resp, at, T, total)
            ggt[:, pl.ds(at, ZR)] = jnp.sum(total, axis=0, keepdims=True)

        def input_grad(source, col, base):
            factor = 1.0 + gain_v[:, pl.ds(hcol, H)]

            def run(i, _):
                spot = pl.ds(pl.multiple_of(i * 16, 16), 16)
                there = pl.ds(pl.multiple_of(base + i * 16, 16), 16)
                scale = inv[there, :][:, :1]
                unit = source[spot, pl.ds(col, H)].astype(F32) * scale
                there_too = pl.ds(pl.multiple_of(T - base + i * 16, 16), 16)
                mean = jnp.sum(rs[there, :] + rsp[there_too, :], axis=1, keepdims=True) * (1.0 / D)
                ig[there, :] = (scale * (dn[there, :] * factor - unit * mean)).astype(BF16)
                return 0

            lax.fori_loop(0, T // 16, run, 0)

        delta_copy = pltpu.make_async_copy(od, delta_o, loc.at[6])
        ig_copy = pltpu.make_async_copy(ig.at[pl.ds(0, T)], igrad_o.at[0, :, pl.ds(hcol, H)], loc.at[7])
        values_copy = pltpu.make_async_copy(vout, values_o.at[0], loc.at[8])
        gain_copy = pltpu.make_async_copy(ggt, ggrad_o.at[:, pl.ds(hcol, H)], loc.at[9])

        def values_send():
            go(vacc.at[pl.ds(T, T)], vrecv, part_s.at[4], part_r.at[4], partner)

        def sums_send():
            go(rs, rsp, part_s.at[5], part_r.at[5], partner)
            ggx[x] = ggt[...]
            for k in range(1, 4):
                go(ggx.at[x], ggx.at[x], gx_s.at[k], gx_r.at[k], dev(q, (x + k) % 4, c))

        def igrad_other():
            got(rsp, part_r.at[5])
            input_grad(resp, 0, T)
            go(ig.at[pl.ds(T, T)], igrad_o.at[0, :, pl.ds(hcol, H)], part_s.at[6], part_r.at[6], partner)

        def igrad_own():
            input_grad(res, hcol, 0)
            ig_copy.start()

        def gain_x():
            for k in range(1, 4):
                got(ggx.at[(x + 4 - k) % 4], gx_r.at[k])
            ggz[q] = (ggx[0] + ggx[1]) + (ggx[2] + ggx[3])
            for k in range(1, 4):
                go(ggz.at[q], ggz.at[q], gz_s.at[k], gz_r.at[k], dev((q + k) % 4, x, c))

        def gain_z():
            for k in range(1, 4):
                got(ggz.at[(q + 4 - k) % 4], gz_r.at[k])
            ggt[...] = (ggz[0] + ggz[1]) + (ggz[2] + ggz[3])
            gain_copy.start()
            go(ggt, ggrad_o.at[:, pl.ds(hcol, H)], part_s.at[7], part_r.at[7], partner)

        def values_end():
            got(vrecv, part_r.at[4])
            vout[...] = ((vacc[pl.ds(0, T), :] + vrecv[...]) * out_scale).astype(BF16)
            values_copy.start()

        def delta_end():
            outer_out()
            delta_copy.start()

        steps = [
            own_in, lambda: ag_z_send(near, 0, owner), lambda: ag_z_send(near, 1, owner),
            lambda: ag_x_send(near, 0, owner), lambda: ag_x_send(near, 1, owner),
            lambda: ax_send(0), lambda: ax_send(1), ax_left, ax_right, ax_end,
            lambda: ax_own(0), lambda: ax_own(1), lambda: ax_own(2), lambda: ax_own(3),
            scales, normed_own, normed_other,
            rx_opp, rx_plain, rx_right, rx_left, rx_end, lambda: grad_out(0), lambda: grad_out(1),
            outer_start, outer_mid, outer_last, delta_end,
            values_send, sums_send, igrad_other, igrad_own, gain_x, gain_z, values_end,
        ]
        for zl, first in ((near, True), (far, False)):
            steps.append(lambda zl=zl: ag_z(zl, 0))
            steps.append(lambda zl=zl: ag_z(zl, 1))
            for run in (
                ag_left, ag_right, ag_end, grad_rows, rs_opp,
                rs_plain, rs_right, rs_left,
            ):
                steps.append(lambda run=run, zl=zl: run(zl))
            for run in (rs_x, rs_z):
                steps.append(lambda run=run, zl=zl: run(zl, 0))
                steps.append(lambda run=run, zl=zl: run(zl, 1))
            steps.append(lambda zl=zl: dnormed(zl))
            steps.append(lambda zl=zl, first=first: near_far_values(zl, first))
            steps.append(lambda zl=zl, first=first: sums(zl, first))
            for run in (ax_z, rx_z):
                for k in range(4):
                    steps.append(lambda run=run, zl=zl, k=k: run(zl, k))

        def finish():
            for k, cols in enumerate((zcols, xcols)):
                got(grad_o.at[:, cols], part_r.at[8 + k], not owner)
            got(igrad_o.at[0, :, pl.ds(pcol, H)], part_r.at[6])
            got(ggrad_o.at[:, pl.ds(pcol, H)], part_r.at[7])
            for item in grad_mine:
                when(owner, lambda item=item: item.wait())
            for item in (delta_copy, ig_copy, values_copy, gain_copy):
                item.wait()
            for cond, made in sends[first_sends:]:
                when(cond, lambda made=made: made.wait_send())

        for number in order:
            step(number, steps[number])
        step(-1, finish)
        del sends[first_sends:]

    for kind, order in enumerate(ORDERS):
        @pl.when(place == kind)
        def _(owner=kind < 2, order=order):
            all_steps(owner, order)

    for cond, made in sends:
        when(cond, lambda made=made: made.wait_send())


def main_call(frag, delay, residual, cotangent, gain, master, anchor, history):
    any_space = pl.BlockSpec(memory_space=pl.ANY)
    smem = pl.BlockSpec(memory_space=pltpu.SMEM)
    vm = pltpu.VMEM
    dma = pltpu.SemaphoreType.DMA
    nx = max(NX, 128)
    scratch = [
        vm((T, D), BF16), vm((T, H), BF16), vm((2 * T, DV), BF16), vm((1, D), F32),
        vm((R, DV), F32), vm((R, DV), F32), vm((HIST, PART, DV), F32),
        vm((H, DV), BF16), vm((R, DV), BF16), vm((H, DV), BF16), vm((2 * T, H), BF16),
        vm((2 * T, 128), F32), vm((2 * T, H), F32), vm((2 * T, DV), F32), vm((T, DV), F32),
        vm((T, DV), BF16), vm((2 * T, 128), F32), vm((2 * T, 128), F32), vm((2 * T, H), BF16),
        vm((4, 1, H), F32), vm((4, 1, H), F32), vm((1, H), F32),
        vm((2, 2, R, NZ), BF16), vm((2, 2, SLOT, NZ), BF16), vm((2, 2, SLOT, NZ), BF16),
        vm((2, 2, 4, SLOT, nx), BF16), vm((2, R, nx), BF16), vm((2, SLOT, nx), BF16),
        vm((PART, DV), F32), vm((4, PART, QUART), F32), vm((PART, QUART), F32),
        vm((PART, QUART), F32), vm((PART, DV), F32),
        dma((12,)), dma((10,)), dma((10,)), dma((2, 2, 2)), dma((2, 2)), dma((2, 6)), dma((2, 6)),
        dma((6,)), dma((6,)), dma((2, 4, 2)), dma((2, 4)),
        dma((2, 6)), dma((2, 6)), dma((2, 2, 2)), dma((2, 2, 2)),
        dma((2, 2, 4)), dma((2, 2, 4)), dma((6,)), dma((6,)),
        dma((4,)), dma((4,)), dma((4,)), dma((4,)),
        dma((4,)), dma((4,)), dma, dma, dma((4,)), dma((4,)),
        pltpu.SemaphoreType.REGULAR, pltpu.SemaphoreType.REGULAR,
    ]
    return pl.pallas_call(
        main_kernel,
        out_shape=(
            jax.ShapeDtypeStruct((1, T, DV), BF16),
            jax.ShapeDtypeStruct((1, T, D), BF16),
            jax.ShapeDtypeStruct((1, D), F32),
            jax.ShapeDtypeStruct((R, DV), BF16),
            jax.ShapeDtypeStruct((PART, DV), F32),
        ),
        in_specs=[smem, smem] + [any_space] * 6,
        out_specs=(any_space,) * 5,
        scratch_shapes=scratch,
        compiler_params=pltpu.CompilerParams(
            collective_id=0, has_side_effects=True, vmem_limit_bytes=44 * 1024 * 1024
        ),
        name="inner_step",
    )(frag, delay, residual, cotangent, gain, master, anchor, history)


def update_kernel(
    frag, grad, delta, master, first, second, anchor, momentum, values, igrad, ggrad,
    master_o, first_o, second_o, anchor_o, momentum_o, values_o, igrad_o, ggrad_o,
    grad_v, delta_v, master_v, first_v, second_v, anchor_v, momentum_v,
    master_n, first_n, second_n, load, load_small, stored, through,
):
    rows = FRAGS * FR_ROWS
    groups = R // rows
    spots = [pl.ds(i * rows, rows) for i in range(groups)]
    small = [
        pltpu.make_async_copy(grad, grad_v, load_small.at[0]),
        pltpu.make_async_copy(delta, delta_v, load_small.at[1]),
    ]
    for item in small:
        item.start()
    loads = []
    for i, at in enumerate(spots):
        loads.append([
            pltpu.make_async_copy(src, dst, load.at[i, k])
            for k, (src, dst) in enumerate((
                (master.at[0, at], master_v.at[at]),
                (first.at[0, at], first_v.at[at]),
                (second.at[0, at], second_v.at[at]),
                (anchor.at[at], anchor_v.at[at]),
                (momentum.at[at], momentum_v.at[at]),
            ))
        ])
    for item in loads[0] + loads[1] + loads[2]:
        item.start()
    passed = [
        pltpu.make_async_copy(src, dst, through.at[k])
        for k, (src, dst) in enumerate(((igrad, igrad_o), (values, values_o), (ggrad, ggrad_o)))
    ]
    for item in passed:
        item.start()
    for item in small:
        item.wait()
    begin = lax.axis_index("fsdp") * (R // FR_ROWS)
    stores = []
    for i, at in enumerate(spots):
        for item in loads[i]:
            item.wait()
        chosen = jnp.int32(0)
        for k in range(1, FRAGS):
            chosen = chosen + jnp.where(frag[begin + i * FRAGS + k] == 0, k, 0)
        block = pl.ds(pl.multiple_of(i * rows + chosen * FR_ROWS, FR_ROWS), FR_ROWS)

        change = delta_v[pl.ds(i * FR_ROWS, FR_ROWS), :]
        anchor_old = anchor_v[block, :]
        momentum_part = outer_beta * momentum_v[block, :] + change
        anchor_part = anchor_old - outer_rate * (change + outer_beta * momentum_part)
        anchor_v[block, :] = anchor_part
        momentum_v[block, :] = momentum_part

        def store(k, src, dst):
            item = pltpu.make_async_copy(src, dst, stored.at[i, k])
            item.start()
            stores.append(item)

        store(0, anchor_v.at[at], anchor_o.at[at])
        store(1, momentum_v.at[at], momentum_o.at[at])
        for piece in range(rows // 16):
            part = pl.ds(i * rows + piece * 16, 16)
            gradient = grad_v[part, :].astype(F32)
            weights = master_v[part, :]
            first_new = beta_one * first_v[part, :] + (1.0 - beta_one) * gradient
            second_new = beta_two * second_v[part, :] + (1.0 - beta_two) * gradient * gradient
            first_n[part, :] = first_new
            second_n[part, :] = second_new
            master_n[part, :] = weights - inner_rate * (
                first_new / (jnp.sqrt(second_new) + adam_eps) + weight_decay * weights
            )
        store(2, first_n.at[at], first_o.at[0, at])
        store(3, second_n.at[at], second_o.at[0, at])
        master_n[block, :] = mix_weight * master_n[block, :] + (1.0 - mix_weight) * anchor_part
        store(4, master_n.at[at], master_o.at[0, at])
    for item in stores + passed:
        item.wait()


def update_call(frag, grad, delta, master, first, second, anchor, momentum, values, igrad, ggrad):
    any_space = pl.BlockSpec(memory_space=pl.ANY)
    like3 = jax.ShapeDtypeStruct((1, R, DV), F32)
    like2 = jax.ShapeDtypeStruct((R, DV), F32)
    dma = pltpu.SemaphoreType.DMA
    whole = pltpu.VMEM((R, DV), F32)
    groups = R // (FRAGS * FR_ROWS)
    return pl.pallas_call(
        update_kernel,
        out_shape=(
            like3, like3, like3, like2, like2,
            jax.ShapeDtypeStruct((1, T, DV), BF16),
            jax.ShapeDtypeStruct((1, T, D), BF16),
            jax.ShapeDtypeStruct((1, D), F32),
        ),
        in_specs=[pl.BlockSpec(memory_space=pltpu.SMEM)] + [any_space] * 10,
        out_specs=(any_space,) * 8,
        scratch_shapes=[pltpu.VMEM((R, DV), BF16), pltpu.VMEM((PART, DV), F32)]
        + [whole] * 8
        + [dma((groups, 5)), dma((2,)), dma((groups, 5)), dma((3,))],
        compiler_params=pltpu.CompilerParams(vmem_limit_bytes=16 * 1024 * 1024),
        name="update",
    )(frag, grad, delta, master, first, second, anchor, momentum, values, igrad, ggrad)


def body(
    residual, cotangent, norm_gain, master, first_moment, second_moment,
    anchor, outer_momentum, history, fragment, delay,
):
    (
        residual, cotangent, norm_gain, master, first_moment, second_moment,
        anchor, outer_momentum, history, fragment, delay,
    ) = [
        pltpu.with_memory_space_constraint(item, pltpu.HBM)
        for item in (
            residual, cotangent, norm_gain, master, first_moment, second_moment,
            anchor, outer_momentum, history, fragment, delay,
        )
    ]
    values, input_grad, gain_grad, gradient, delta = main_call(
        fragment, delay, residual, cotangent, norm_gain, master, anchor, history
    )
    new_master, new_first, new_second, new_anchor, new_momentum, values, input_grad, gain_grad = update_call(
        fragment, gradient, delta, master, first_moment, second_moment, anchor, outer_momentum,
        values, input_grad, gain_grad,
    )
    return (
        values, input_grad, gain_grad, new_master, new_first, new_second, new_anchor, new_momentum,
    )


def solution(mesh):
    rows = P("replica", "fsdp", None)
    both = P("fsdp", None)
    return jax.shard_map(
        body,
        mesh=mesh,
        in_specs=(
            rows, rows, P("replica", None), rows, rows, rows, both, both,
            P("replica", None, "fsdp", None), P(), P("replica", "fsdp"),
        ),
        out_specs=(rows, rows, P("replica", None), rows, rows, rows, both, both),
        check_vma=False,
    )
```

```python
import jax
import jax.numpy as jnp
from jax import lax
from jax.experimental import pallas as pl
from jax.experimental.pallas import tpu as pltpu
from jax.sharding import PartitionSpec as P

D = 4608
DV = 1024
FRAGS = 6
FR_ROWS = 8
HIST = 4

T = 256
R = 144
SLOT = 2 * R
ZR = 4 * SLOT
H = 2 * ZR
TILE = 384
NZ = 640
NX = DV - NZ
PART = R // FRAGS
QUART = DV // 4

norm_eps = 1e-06
beta_one = 0.9
beta_two = 0.95
inner_rate = 0.01
weight_decay = 0.1
adam_eps = 1e-08
outer_beta = 0.9
outer_rate = 0.7
mix_weight = 0.5
out_scale = float(D) ** (-0.5)

MESH = pl.DeviceIdType.MESH
F32 = jnp.float32
BF16 = jnp.bfloat16


ORDERS = [
    [
        1, 5, 0, 10, 6, 4, 14, 3, 2, 60, 8, 12, 7, 11, 61, 37, 38, 9, 78, 13, 16, 39, 15, 77, 79, 24, 62, 63,
        50, 49, 80, 65, 64, 40, 51, 82, 25, 84, 66, 74, 81, 68, 41, 83, 26, 67, 76, 69, 75, 29, 42, 27, 44,
        70, 56, 43, 57, 71, 32, 73, 72, 58, 59, 17, 30, 28, 18, 19, 20, 46, 31, 33, 48, 34, 45, 47, 22, 21,
        23,
    ],
    [
        1, 5, 24, 0, 6, 2, 10, 4, 60, 8, 7, 11, 3, 14, 12, 61, 16, 78, 15, 37, 38, 9, 25, 13, 77, 79, 40, 39,
        65, 50, 62, 63, 80, 49, 64, 74, 66, 67, 51, 83, 75, 81, 69, 82, 68, 41, 76, 28, 26, 29, 84, 56, 57,
        42, 58, 30, 59, 17, 71, 70, 44, 43, 18, 73, 32, 31, 72, 20, 19, 27, 34, 45, 46, 47, 48, 33, 22, 21,
        23,
    ],
    [
        14, 35, 15, 16, 36, 65, 60, 53, 40, 54, 67, 61, 37, 52, 66, 38, 55, 83, 78, 63, 69, 77, 41, 81, 62,
        39, 24, 58, 68, 79, 82, 57, 49, 42, 80, 51, 84, 50, 43, 44, 56, 25, 71, 59, 64, 73, 74, 76, 45, 70,
        26, 29, 46, 75, 72, 47, 28, 30, 48, 32, 33, 27, 34, 31,
    ],
    [
        14, 15, 16, 40, 41, 65, 66, 83, 84, 24, 35, 25, 57, 43, 69, 81, 36, 58, 82, 67, 68, 53, 56, 38, 54,
        60, 37, 59, 61, 71, 26, 73, 44, 55, 39, 52, 27, 42, 63, 49, 62, 70, 77, 51, 50, 46, 72, 45, 64, 47,
        79, 48, 78, 80, 74, 76, 29, 75, 30, 32, 31, 28, 33, 34,
    ],
]


def step(number, run):
    run()


def main_kernel(
    frag, delay, residual, cotangent, gain, master, anchor, history, first, second, momentum,
    values_o, igrad_o, ggrad_o, grad_o, delta_o, master_c, first_c, second_c, anchor_c, momentum_c,
    res, resp, cot, gain_v, master_v, anchor_v, hist_v,
    wh, stage, g, normed, inv, dn, vacc, vrecv, vout, rs, rsp, ig, ggx, ggz, ggt,
    opp, full, zbuf, zxbuf, oppx, fullx, oterm, obuf, osum, ozh, od,
    loc, part_s, part_r, agz_s, agz_r, agx_s, agx_r, axx_s, axx_r, axz_s, axz_r,
    rsx_s, rsx_r, rsz_s, rsz_r, rxz_s, rxz_r, rxx_s, rxx_r, gx_s, gx_r, gz_s, gz_r,
    oy_s, oy_r, oz_s, oz_r, ob_s, ob_r, ready_y, ready_z,
):
    me = lax.axis_index("fsdp")
    rep = lax.axis_index("replica")
    q, x, c = me // 8, (me // 2) % 4, me % 2
    y, zh = rep // 2, rep % 2
    xr, xl, xo = (x + 1) % 4, (x + 3) % 4, (x + 2) % 4
    handler = c == q // 2
    place = jnp.where(c == 0, q, 3 - q)
    near = jnp.where(place == 0, c, 1 - c)
    far = 1 - near

    def dev(qq, xx, cc):
        return {"fsdp": qq * 8 + xx * 2 + cc}

    partner, right, left = dev(q, x, 1 - c), dev(q, xr, c), dev(q, xl, c)
    up, down = dev(q + 1, x, c), dev(q - 1, x, c)

    sends = []

    def copy(src, dst, send, recv, to):
        return pltpu.make_async_remote_copy(
            src_ref=src, dst_ref=dst, send_sem=send, recv_sem=recv, device_id=to, device_id_type=MESH
        )

    def when(cond, run):
        if cond is True:
            run()
        elif cond is not False:
            @pl.when(cond)
            def _():
                run()

    def go(src, dst, send, recv, to, cond=True):
        made = copy(src, dst, send, recv, to)
        when(cond, lambda: made.start())
        sends.append((cond, made))

    def got(dst, recv, cond=True):
        made = copy(dst, dst, part_s.at[0], recv, partner)
        when(cond, lambda: made.wait_recv())

    local_in = [
        pltpu.make_async_copy(master.at[0], master_v, loc.at[0]),
        pltpu.make_async_copy(residual.at[0], res, loc.at[1]),
        pltpu.make_async_copy(cotangent.at[0], cot.at[pl.ds(0, T)], loc.at[2]),
        pltpu.make_async_copy(gain, gain_v, loc.at[3]),
        pltpu.make_async_copy(anchor, anchor_v, loc.at[4]),
        pltpu.make_async_copy(history.at[0], hist_v, loc.at[5]),
    ]
    for item in local_in:
        item.start()

    carried = [
        pltpu.make_async_copy(src, dst, loc.at[12 + k])
        for k, (src, dst) in enumerate((
            (master.at[0], master_c), (first.at[0], first_c), (second.at[0], second_c),
            (anchor, anchor_c), (momentum, momentum_c),
        ))
    ]

    barrier = pltpu.get_barrier_semaphore()
    greeted = [partner]
    greeted += [dev(q, (x + k) % 4, c) for k in range(1, 4)]
    greeted += [dev((q + k) % 4, x, c) for k in range(1, 4)]
    for to in greeted:
        pl.semaphore_signal(barrier, inc=1, device_id=to, device_id_type=MESH)

    other_z = {"replica": y * 2 + 1 - zh}

    @pl.when(zh == 0)
    def _():
        pl.semaphore_signal(barrier, inc=1, device_id=other_z, device_id_type=MESH)

    for k in range(1, 4):
        @pl.when(y + k < 4)
        def _(k=k):
            pl.semaphore_signal(
                barrier, inc=1, device_id={"replica": (y + k) * 2 + zh}, device_id_type=MESH
            )

    own = q % 2
    local_in[0].wait()
    own_rows = pl.ds(pl.multiple_of(own * ZR + x * SLOT + c * R, 16), R)

    @pl.when(handler)
    def _():
        wh[own_rows, :] = master_v[...].astype(BF16)

    @pl.when(jnp.logical_not(handler))
    def _():
        stage[...] = master_v[...].astype(BF16)

    pl.semaphore_wait(barrier, len(greeted) + y + zh)

    @pl.when(zh == 1)
    def _():
        pl.semaphore_signal(ready_z, inc=1, device_id=other_z, device_id_type=MESH)

    for k in range(1, 4):
        @pl.when(y >= k)
        def _(k=k):
            pl.semaphore_signal(
                ready_y, inc=1, device_id={"replica": (y - k) * 2 + zh}, device_id_type=MESH
            )

    zcols, xcols = pl.ds(0, NZ), pl.ds(NZ, NX)

    def rows(zl, xx, half=0):
        return pl.multiple_of(zl * ZR + xx * SLOT + half * R, 16)

    def block(buf, zl, xx, cols, half=None):
        if half is None:
            return buf.at[pl.ds(rows(zl, xx), SLOT), cols]
        return buf.at[pl.ds(rows(zl, xx, half), R), cols]

    hcol = pl.multiple_of(c * H, 128)
    pcol = pl.multiple_of((1 - c) * H, 128)

    go(stage, wh.at[own_rows, :], part_s.at[0], part_r.at[0], partner, jnp.logical_not(handler))
    other_rows = pl.ds(pl.multiple_of(own * ZR + x * SLOT + (1 - c) * R, 16), R)

    go(residual.at[0, :, pl.ds(pcol, H)], resp, part_s.at[1], part_r.at[1], partner)
    go(cotangent.at[0], cot.at[pl.ds(T, T)], part_s.at[2], part_r.at[2], partner)

    first_sends = len(sends)

    for item in carried:
        item.start()

    def all_steps(owner, order):
        def slot_of(k):
            return (x, xl, xr, xo)[k]

        def towards(zl):
            goal = 2 * c + zl
            return jnp.logical_and(q >= goal, q < 3), jnp.logical_and(q <= goal, q > 0)

        def both(fixed, cond):
            return cond if fixed else False

        def own_in():
            got(wh.at[other_rows, :], part_r.at[0], owner)

        def turn(h):
            return c if h == 0 else 1 - c

        def ag_z_send(zl, h, cond):
            ref = block(wh, zl, x, zcols, turn(h))
            go_up, go_down = towards(zl)
            go(ref, ref, agz_s.at[zl, 0, h], agz_r.at[zl, h], up, both(cond, go_up))
            go(ref, ref, agz_s.at[zl, 1, h], agz_r.at[zl, h], down, both(cond, go_down))

        def ag_x_send(zl, h, cond):
            ref = block(wh, zl, x, zcols, turn(h))
            go(ref, ref, agx_s.at[zl, turn(h)], agx_r.at[zl, turn(h)], right, cond)
            go(ref, ref, agx_s.at[zl, 2 + turn(h)], agx_r.at[zl, 2 + turn(h)], left, cond)

        def ag_z(zl, h):
            cond = not (owner and zl is near)
            got(block(wh, zl, x, zcols, turn(h)), agz_r.at[zl, h], cond)
            ag_z_send(zl, h, cond)
            ag_x_send(zl, h, cond)

        def ag_left(zl):
            ref = block(wh, zl, xl, zcols, 0)
            got(ref, agx_r.at[zl, 0])
            go(ref, ref, agx_s.at[zl, 4], agx_r.at[zl, 4], right)

        def ag_right(zl):
            ref = block(wh, zl, xr, zcols, 1)
            got(ref, agx_r.at[zl, 3])
            go(ref, ref, agx_s.at[zl, 5], agx_r.at[zl, 5], left)

        def ag_end(zl):
            got(block(wh, zl, xl, zcols, 1), agx_r.at[zl, 1])
            got(block(wh, zl, xr, zcols, 0), agx_r.at[zl, 2])
            got(block(wh, zl, xo, zcols, 0), agx_r.at[zl, 4])
            got(block(wh, zl, xo, zcols, 1), agx_r.at[zl, 5])

        def ax_send(h):
            ref = block(wh, own, x, xcols, turn(h))
            go(ref, ref, axx_s.at[h], axx_r.at[h], right, owner)
            go(ref, ref, axx_s.at[2 + h], axx_r.at[2 + h], left, owner)

        def ax_left():
            ref = block(wh, own, xl, xcols, 0)
            got(ref, axx_r.at[c], owner)
            go(ref, ref, axx_s.at[4], axx_r.at[4], right, owner)

        def ax_right():
            ref = block(wh, own, xr, xcols, 1)
            got(ref, axx_r.at[3 - c], owner)
            go(ref, ref, axx_s.at[5], axx_r.at[5], left, owner)

        def ax_end():
            got(block(wh, own, xo, xcols, 0), axx_r.at[4], owner)
            got(block(wh, own, xo, xcols, 1), axx_r.at[5], owner)

        def ax_z_send(zl, k, cond):
            ref = block(wh, zl, slot_of(k), xcols)
            go_up, go_down = towards(zl)
            go(ref, ref, axz_s.at[zl, k, 0], axz_r.at[zl, k], up, both(cond, go_up))
            go(ref, ref, axz_s.at[zl, k, 1], axz_r.at[zl, k], down, both(cond, go_down))

        def ax_own(k):
            if k == 1:
                got(block(wh, own, xl, xcols, 1), axx_r.at[1 - c], owner)
            if k == 2:
                got(block(wh, own, xr, xcols, 0), axx_r.at[2 + c], owner)
            ax_z_send(near, k, owner)

        def ax_z(zl, k):
            cond = not (owner and zl is near)
            got(block(wh, zl, slot_of(k), xcols), axz_r.at[zl, k], cond)
            ax_z_send(zl, k, cond)

        def norm_rows(i, _):
            spot = pl.ds(pl.multiple_of(i * 16, 16), 16)
            raw = res[spot, :].astype(F32)
            scale = lax.rsqrt(jnp.mean(raw * raw, axis=1, keepdims=True) + norm_eps)
            inv[spot, :] = jnp.broadcast_to(scale, (16, 128))
            return 0

        def scales():
            local_in[3].wait()
            local_in[1].wait()
            lax.fori_loop(0, T // 16, norm_rows, 0)
            go(inv.at[pl.ds(0, T)], inv.at[pl.ds(T, T)], part_s.at[3], part_r.at[3], partner)

        def normed_rows(source, col, base):
            def run(i, _):
                spot = pl.ds(pl.multiple_of(i * 16, 16), 16)
                there = pl.ds(pl.multiple_of(base + i * 16, 16), 16)
                scale = inv[there, :][:, :1]
                factor = 1.0 + gain_v[:, pl.ds(hcol, H)]
                raw = source[spot, pl.ds(col, H)].astype(F32)
                normed[there, :] = (raw * scale * factor).astype(BF16)
                return 0

            lax.fori_loop(0, T // 16, run, 0)

        def normed_own():
            normed_rows(res, hcol, 0)

        def normed_other():
            got(inv.at[pl.ds(T, T)], part_r.at[3])
            got(resp, part_r.at[1])
            normed_rows(resp, 0, T)
            local_in[2].wait()
            got(cot.at[pl.ds(T, T)], part_r.at[2])

        def grad_rows(zl):
            def run(t, _):
                at = zl * ZR + t * TILE
                a = normed[:, pl.ds(pl.multiple_of(at, 128), TILE)]
                part = lax.dot_general(a, cot[...], (((0,), (0,)), ((), ())), preferred_element_type=F32)
                g[pl.ds(pl.multiple_of(at, 16), TILE), :] = (part * out_scale).astype(BF16)
                return 0

            lax.fori_loop(0, ZR // TILE, run, 0)

        def add_into(row, count, cols, terms, cond=True):
            step = 48

            def run(i, _):
                spot = pl.ds(pl.multiple_of(row + i * step, 16), step)
                here = pl.ds(pl.multiple_of(i * step, 16), step)
                total = g[spot, cols].astype(F32)
                for term in terms:
                    total = total + term[here, :].astype(F32)
                g[spot, cols] = total.astype(BF16)
                return 0

            when(cond, lambda: lax.fori_loop(0, count // step, run, 0))

        def rs_opp(zl):
            go(block(g, zl, xo, zcols, 0), opp.at[zl, 0], rsx_s.at[zl, 0], rsx_r.at[zl, 0], right)
            go(block(g, zl, xo, zcols, 1), opp.at[zl, 1], rsx_s.at[zl, 1], rsx_r.at[zl, 1], left)

        first_half, second_half = pl.ds(0, R), pl.ds(R, R)

        def rs_plain(zl):
            go(block(g, zl, xr, zcols, 1), full.at[zl, 0, second_half], rsx_s.at[zl, 4], rsx_r.at[zl, 4], right)
            go(block(g, zl, xl, zcols, 0), full.at[zl, 1, first_half], rsx_s.at[zl, 5], rsx_r.at[zl, 5], left)

        def rs_right(zl):
            got(opp.at[zl, 0], rsx_r.at[zl, 0])
            add_into(rows(zl, xr, 0), R, zcols, [opp.at[zl, 0]])
            go(block(g, zl, xr, zcols, 0), full.at[zl, 0, first_half], rsx_s.at[zl, 2], rsx_r.at[zl, 2], right)

        def rs_left(zl):
            got(opp.at[zl, 1], rsx_r.at[zl, 1])
            add_into(rows(zl, xl, 1), R, zcols, [opp.at[zl, 1]])
            go(block(g, zl, xl, zcols, 1), full.at[zl, 1, second_half], rsx_s.at[zl, 3], rsx_r.at[zl, 3], left)

        def rs_x(zl, h):
            part = (first_half, second_half)[h]
            got(full.at[zl, 0, part], rsx_r.at[zl, (2, 4)[h]])
            got(full.at[zl, 1, part], rsx_r.at[zl, (5, 3)[h]])
            add_into(rows(zl, x, h), R, zcols, [full.at[zl, 0, part], full.at[zl, 1, part]])

        def rs_z(zl, h):
            above, below = towards(zl)
            goal = 2 * c + zl
            high = zbuf.at[zl, 1, pl.ds(h * R, R)]
            low = zbuf.at[zl, 0, pl.ds(h * R, R)]
            got(high, rsz_r.at[zl, 1, h], above)
            add_into(rows(zl, x, h), R, zcols, [high], above)
            got(low, rsz_r.at[zl, 0, h], below)
            add_into(rows(zl, x, h), R, zcols, [low], below)
            ref = block(g, zl, x, zcols, h)
            go(ref, high, rsz_s.at[zl, 0, h], rsz_r.at[zl, 1, h], down, q > goal)
            go(ref, low, rsz_s.at[zl, 1, h], rsz_r.at[zl, 0, h], up, q < goal)

        def rx_z(zl, k):
            above, below = towards(zl)
            xx = slot_of(k)
            got(zxbuf.at[zl, 1, k], rxz_r.at[zl, 1, k], above)
            add_into(rows(zl, xx), SLOT, xcols, [zxbuf.at[zl, 1, k]], above)
            got(zxbuf.at[zl, 0, k], rxz_r.at[zl, 0, k], below)
            add_into(rows(zl, xx), SLOT, xcols, [zxbuf.at[zl, 0, k]], below)
            ref = block(g, zl, xx, xcols)
            goal = 2 * c + zl
            go(ref, zxbuf.at[zl, 1, k], rxz_s.at[zl, 0, k], rxz_r.at[zl, 1, k], down, q > goal)
            go(ref, zxbuf.at[zl, 0, k], rxz_s.at[zl, 1, k], rxz_r.at[zl, 0, k], up, q < goal)

        def rx_opp():
            go(block(g, own, xo, xcols, 0), oppx.at[0], rxx_s.at[0], rxx_r.at[0], right, owner)
            go(block(g, own, xo, xcols, 1), oppx.at[1], rxx_s.at[1], rxx_r.at[1], left, owner)

        def rx_plain():
            go(block(g, own, xr, xcols, 1), fullx.at[0, second_half], rxx_s.at[4], rxx_r.at[4], right, owner)
            go(block(g, own, xl, xcols, 0), fullx.at[1, first_half], rxx_s.at[5], rxx_r.at[5], left, owner)

        def rx_right():
            got(oppx.at[0], rxx_r.at[0], owner)
            add_into(rows(own, xr, 0), R, xcols, [oppx.at[0]], owner)
            go(block(g, own, xr, xcols, 0), fullx.at[0, first_half], rxx_s.at[2], rxx_r.at[2], right, owner)

        def rx_left():
            got(oppx.at[1], rxx_r.at[1], owner)
            add_into(rows(own, xl, 1), R, xcols, [oppx.at[1]], owner)
            go(block(g, own, xl, xcols, 1), fullx.at[1, second_half], rxx_s.at[3], rxx_r.at[3], left, owner)

        def rx_end():
            for h, part in ((0, first_half), (1, second_half)):
                got(fullx.at[0, part], rxx_r.at[(2, 4)[h]], owner)
                got(fullx.at[1, part], rxx_r.at[(5, 3)[h]], owner)
                add_into(rows(own, x, h), R, xcols, [fullx.at[0, part], fullx.at[1, part]], owner)

        grad_mine = [
            pltpu.make_async_copy(g.at[own_rows, cols], grad_o.at[:, cols], loc.at[10 + k])
            for k, cols in enumerate((zcols, xcols))
        ]

        def grad_out(k):
            cols = (zcols, xcols)[k]
            when(owner, lambda: grad_mine[k].start())
            go(g.at[other_rows, cols], grad_o.at[:, cols], part_s.at[8 + k], part_r.at[8 + k], partner, owner)

        def outer_start():
            local_in[4].wait()
            local_in[5].wait()
            for b in range(R // (FRAGS * FR_ROWS)):
                first = me * (R // FR_ROWS) + b * FRAGS
                spot = pl.ds(b * FR_ROWS, FR_ROWS)
                term = jnp.zeros((FR_ROWS, DV), F32)
                for k in range(FRAGS):
                    taken = (frag[first + k] == 0).astype(F32)
                    term = term + taken * anchor_v[pl.ds((b * FRAGS + k) * FR_ROWS, FR_ROWS), :]
                for k in range(HIST):
                    taken = (delay[0, b] == k + 1).astype(F32)
                    term = term - taken * hist_v[k, spot, :]
                oterm[spot, :] = term
            @pl.when(y < 3)
            def _():
                pl.semaphore_wait(ready_y, 3 - y)

            obuf[y] = oterm[:, pl.ds(pl.multiple_of(y * QUART, 128), QUART)]
            for k in range(1, 4):
                yy = (y + k) % 4
                go(
                    oterm.at[:, pl.ds(pl.multiple_of(yy * QUART, 128), QUART)], obuf.at[y],
                    oy_s.at[k], oy_r.at[k], {"replica": yy * 2 + zh},
                )

        def outer_mid():
            for k in range(1, 4):
                got(obuf.at[(y + 4 - k) % 4], oy_r.at[k])
            osum[...] = (obuf[0] + obuf[1]) + (obuf[2] + obuf[3])
            @pl.when(zh == 0)
            def _():
                pl.semaphore_wait(ready_z, 1)

            go(osum, ozh, oz_s, oz_r, other_z)

        def outer_last():
            got(ozh, oz_r)
            mine = pl.ds(pl.multiple_of(y * QUART, 128), QUART)
            od[:, mine] = (osum[...] + ozh[...]) * 0.125
            for k in range(1, 4):
                go(od.at[:, mine], od.at[:, mine], ob_s.at[k], ob_r.at[k], {"replica": ((y + k) % 4) * 2 + zh})

        def outer_out():
            for k in range(1, 4):
                theirs = pl.ds(pl.multiple_of(((y + 4 - k) % 4) * QUART, 128), QUART)
                got(od.at[:, theirs], ob_r.at[k])

        def near_far_values(zl, first):
            def run(n, _):
                cols = pl.ds(pl.multiple_of(n * 256, 128), 256)
                part = jnp.dot(
                    normed[:, pl.ds(pl.multiple_of(zl * ZR, 128), ZR)],
                    wh[pl.ds(pl.multiple_of(zl * ZR, 16), ZR), cols],
                    preferred_element_type=F32,
                )
                if first:
                    vacc[:, cols] = part
                else:
                    vacc[:, cols] = vacc[:, cols] + part
                return 0

            lax.fori_loop(0, DV // 256, run, 0)

        def dnormed(zl):
            def run(t, _):
                at = zl * ZR + t * TILE
                part = lax.dot_general(
                    cot[...], wh[pl.ds(pl.multiple_of(at, 16), TILE), :], (((1,), (1,)), ((), ())),
                    preferred_element_type=F32,
                )
                dn[:, pl.ds(pl.multiple_of(at, 128), TILE)] = part * out_scale
                return 0

            lax.fori_loop(0, ZR // TILE, run, 0)

        def sums(zl, first):
            at = pl.multiple_of(zl * ZR, 128)
            factor = 1.0 + gain_v[:, pl.ds(pl.multiple_of(hcol + at, 128), ZR)]

            def part_of(source, col, base, total):
                def run(i, total):
                    spot = pl.ds(pl.multiple_of(i * 16, 16), 16)
                    there = pl.ds(pl.multiple_of(base + i * 16, 16), 16)
                    unit = source[spot, pl.ds(col, ZR)].astype(F32) * inv[there, :][:, :1]
                    prod = dn[there, pl.ds(at, ZR)] * unit
                    scaled = prod * factor
                    lanes = scaled[:, :128]
                    for k in range(1, ZR // 128):
                        lanes = lanes + scaled[:, k * 128 : (k + 1) * 128]
                    if first:
                        rs[there, :] = lanes
                    else:
                        rs[there, :] = rs[there, :] + lanes
                    return total + (prod[:8] + prod[8:])

                return lax.fori_loop(0, T // 16, run, total)

            total = jnp.zeros((8, ZR), F32)
            total = part_of(res, pl.multiple_of(hcol + at, 128), 0, total)
            total = part_of(resp, at, T, total)
            ggt[:, pl.ds(at, ZR)] = jnp.sum(total, axis=0, keepdims=True)

        def input_grad(source, col, base):
            factor = 1.0 + gain_v[:, pl.ds(hcol, H)]

            def run(i, _):
                spot = pl.ds(pl.multiple_of(i * 16, 16), 16)
                there = pl.ds(pl.multiple_of(base + i * 16, 16), 16)
                scale = inv[there, :][:, :1]
                unit = source[spot, pl.ds(col, H)].astype(F32) * scale
                there_too = pl.ds(pl.multiple_of(T - base + i * 16, 16), 16)
                mean = jnp.sum(rs[there, :] + rsp[there_too, :], axis=1, keepdims=True) * (1.0 / D)
                ig[there, :] = (scale * (dn[there, :] * factor - unit * mean)).astype(BF16)
                return 0

            lax.fori_loop(0, T // 16, run, 0)

        delta_copy = pltpu.make_async_copy(od, delta_o, loc.at[6])
        ig_copy = pltpu.make_async_copy(ig.at[pl.ds(0, T)], igrad_o.at[0, :, pl.ds(hcol, H)], loc.at[7])
        values_copy = pltpu.make_async_copy(vout, values_o.at[0], loc.at[8])
        gain_copy = pltpu.make_async_copy(ggt, ggrad_o.at[:, pl.ds(hcol, H)], loc.at[9])

        def values_send():
            go(vacc.at[pl.ds(T, T)], vrecv, part_s.at[4], part_r.at[4], partner)

        def sums_send():
            go(rs, rsp, part_s.at[5], part_r.at[5], partner)
            ggx[x] = ggt[...]
            for k in range(1, 4):
                go(ggx.at[x], ggx.at[x], gx_s.at[k], gx_r.at[k], dev(q, (x + k) % 4, c))

        def igrad_other():
            got(rsp, part_r.at[5])
            input_grad(resp, 0, T)
            go(ig.at[pl.ds(T, T)], igrad_o.at[0, :, pl.ds(hcol, H)], part_s.at[6], part_r.at[6], partner)

        def igrad_own():
            input_grad(res, hcol, 0)
            ig_copy.start()

        def gain_x():
            for k in range(1, 4):
                got(ggx.at[(x + 4 - k) % 4], gx_r.at[k])
            ggz[q] = (ggx[0] + ggx[1]) + (ggx[2] + ggx[3])
            for k in range(1, 4):
                go(ggz.at[q], ggz.at[q], gz_s.at[k], gz_r.at[k], dev((q + k) % 4, x, c))

        def gain_z():
            for k in range(1, 4):
                got(ggz.at[(q + 4 - k) % 4], gz_r.at[k])
            ggt[...] = (ggz[0] + ggz[1]) + (ggz[2] + ggz[3])
            gain_copy.start()
            go(ggt, ggrad_o.at[:, pl.ds(hcol, H)], part_s.at[7], part_r.at[7], partner)

        def values_end():
            got(vrecv, part_r.at[4])
            vout[...] = ((vacc[pl.ds(0, T), :] + vrecv[...]) * out_scale).astype(BF16)
            values_copy.start()

        def delta_end():
            outer_out()
            delta_copy.start()

        steps = [
            own_in, lambda: ag_z_send(near, 0, owner), lambda: ag_z_send(near, 1, owner),
            lambda: ag_x_send(near, 0, owner), lambda: ag_x_send(near, 1, owner),
            lambda: ax_send(0), lambda: ax_send(1), ax_left, ax_right, ax_end,
            lambda: ax_own(0), lambda: ax_own(1), lambda: ax_own(2), lambda: ax_own(3),
            scales, normed_own, normed_other,
            rx_opp, rx_plain, rx_right, rx_left, rx_end, lambda: grad_out(0), lambda: grad_out(1),
            outer_start, outer_mid, outer_last, delta_end,
            values_send, sums_send, igrad_other, igrad_own, gain_x, gain_z, values_end,
        ]
        for zl, first in ((near, True), (far, False)):
            steps.append(lambda zl=zl: ag_z(zl, 0))
            steps.append(lambda zl=zl: ag_z(zl, 1))
            for run in (
                ag_left, ag_right, ag_end, grad_rows, rs_opp,
                rs_plain, rs_right, rs_left,
            ):
                steps.append(lambda run=run, zl=zl: run(zl))
            for run in (rs_x, rs_z):
                steps.append(lambda run=run, zl=zl: run(zl, 0))
                steps.append(lambda run=run, zl=zl: run(zl, 1))
            steps.append(lambda zl=zl: dnormed(zl))
            steps.append(lambda zl=zl, first=first: near_far_values(zl, first))
            steps.append(lambda zl=zl, first=first: sums(zl, first))
            for run in (ax_z, rx_z):
                for k in range(4):
                    steps.append(lambda run=run, zl=zl, k=k: run(zl, k))

        def finish():
            for k, cols in enumerate((zcols, xcols)):
                got(grad_o.at[:, cols], part_r.at[8 + k], not owner)
            got(igrad_o.at[0, :, pl.ds(pcol, H)], part_r.at[6])
            got(ggrad_o.at[:, pl.ds(pcol, H)], part_r.at[7])
            for item in grad_mine:
                when(owner, lambda item=item: item.wait())
            for item in (delta_copy, ig_copy, values_copy, gain_copy):
                item.wait()
            for cond, made in sends[first_sends:]:
                when(cond, lambda made=made: made.wait_send())

        for number in order:
            step(number, steps[number])
        step(-1, finish)
        del sends[first_sends:]

    for kind, order in enumerate(ORDERS):
        @pl.when(place == kind)
        def _(owner=kind < 2, order=order):
            all_steps(owner, order)

    for item in carried:
        item.wait()
    for cond, made in sends:
        when(cond, lambda made=made: made.wait_send())


def main_call(frag, delay, residual, cotangent, gain, master, anchor, history, first, second, momentum):
    any_space = pl.BlockSpec(memory_space=pl.ANY)
    smem = pl.BlockSpec(memory_space=pltpu.SMEM)
    vm = pltpu.VMEM
    dma = pltpu.SemaphoreType.DMA
    nx = max(NX, 128)
    scratch = [
        vm((T, D), BF16), vm((T, H), BF16), vm((2 * T, DV), BF16), vm((1, D), F32),
        vm((R, DV), F32), vm((R, DV), F32), vm((HIST, PART, DV), F32),
        vm((H, DV), BF16), vm((R, DV), BF16), vm((H, DV), BF16), vm((2 * T, H), BF16),
        vm((2 * T, 128), F32), vm((2 * T, H), F32), vm((2 * T, DV), F32), vm((T, DV), F32),
        vm((T, DV), BF16), vm((2 * T, 128), F32), vm((2 * T, 128), F32), vm((2 * T, H), BF16),
        vm((4, 1, H), F32), vm((4, 1, H), F32), vm((1, H), F32),
        vm((2, 2, R, NZ), BF16), vm((2, 2, SLOT, NZ), BF16), vm((2, 2, SLOT, NZ), BF16),
        vm((2, 2, 4, SLOT, nx), BF16), vm((2, R, nx), BF16), vm((2, SLOT, nx), BF16),
        vm((PART, DV), F32), vm((4, PART, QUART), F32), vm((PART, QUART), F32),
        vm((PART, QUART), F32), vm((PART, DV), F32),
        dma((17,)), dma((10,)), dma((10,)), dma((2, 2, 2)), dma((2, 2)), dma((2, 6)), dma((2, 6)),
        dma((6,)), dma((6,)), dma((2, 4, 2)), dma((2, 4)),
        dma((2, 6)), dma((2, 6)), dma((2, 2, 2)), dma((2, 2, 2)),
        dma((2, 2, 4)), dma((2, 2, 4)), dma((6,)), dma((6,)),
        dma((4,)), dma((4,)), dma((4,)), dma((4,)),
        dma((4,)), dma((4,)), dma, dma, dma((4,)), dma((4,)),
        pltpu.SemaphoreType.REGULAR, pltpu.SemaphoreType.REGULAR,
    ]
    return pl.pallas_call(
        main_kernel,
        out_shape=(
            jax.ShapeDtypeStruct((1, T, DV), BF16),
            jax.ShapeDtypeStruct((1, T, D), BF16),
            jax.ShapeDtypeStruct((1, D), F32),
            jax.ShapeDtypeStruct((R, DV), BF16),
            jax.ShapeDtypeStruct((PART, DV), F32),
        ) + (jax.ShapeDtypeStruct((R, DV), F32),) * 5,
        in_specs=[smem, smem] + [any_space] * 9,
        out_specs=(any_space,) * 10,
        scratch_shapes=scratch,
        compiler_params=pltpu.CompilerParams(
            collective_id=0, has_side_effects=True, vmem_limit_bytes=44 * 1024 * 1024
        ),
        name="inner_step",
    )(frag, delay, residual, cotangent, gain, master, anchor, history, first, second, momentum)


def update_kernel(
    frag, grad_v, delta_v, master_v, first_v, second_v, anchor_v, momentum_v, values, igrad, ggrad,
    master_o, first_o, second_o, anchor_o, momentum_o, values_o, igrad_o, ggrad_o,
    master_n, first_n, second_n, anchor_n, momentum_n, stored, through,
):
    rows = FRAGS * FR_ROWS
    groups = R // rows
    spots = [pl.ds(i * rows, rows) for i in range(groups)]
    passed = [
        pltpu.make_async_copy(src, dst, through.at[k])
        for k, (src, dst) in enumerate(((igrad, igrad_o), (values, values_o), (ggrad, ggrad_o)))
    ]
    for item in passed:
        item.start()
    begin = lax.axis_index("fsdp") * (R // FR_ROWS)
    stores = []
    for i, at in enumerate(spots):
        chosen = jnp.int32(0)
        for k in range(1, FRAGS):
            chosen = chosen + jnp.where(frag[begin + i * FRAGS + k] == 0, k, 0)
        block = pl.ds(pl.multiple_of(i * rows + chosen * FR_ROWS, FR_ROWS), FR_ROWS)

        change = delta_v[pl.ds(i * FR_ROWS, FR_ROWS), :]
        anchor_old = anchor_v[block, :]
        momentum_part = outer_beta * momentum_v[block, :] + change
        anchor_part = anchor_old - outer_rate * (change + outer_beta * momentum_part)
        anchor_n[at, :] = anchor_v[at, :]
        momentum_n[at, :] = momentum_v[at, :]
        anchor_n[block, :] = anchor_part
        momentum_n[block, :] = momentum_part

        def store(k, src, dst):
            item = pltpu.make_async_copy(src, dst, stored.at[i, k])
            item.start()
            stores.append(item)

        store(0, anchor_n.at[at], anchor_o.at[at])
        store(1, momentum_n.at[at], momentum_o.at[at])
        for piece in range(rows // 16):
            part = pl.ds(i * rows + piece * 16, 16)
            gradient = grad_v[part, :].astype(F32)
            weights = master_v[part, :]
            first_new = beta_one * first_v[part, :] + (1.0 - beta_one) * gradient
            second_new = beta_two * second_v[part, :] + (1.0 - beta_two) * gradient * gradient
            first_n[part, :] = first_new
            second_n[part, :] = second_new
            master_n[part, :] = weights - inner_rate * (
                first_new / (jnp.sqrt(second_new) + adam_eps) + weight_decay * weights
            )
        store(2, first_n.at[at], first_o.at[0, at])
        store(3, second_n.at[at], second_o.at[0, at])
        master_n[block, :] = mix_weight * master_n[block, :] + (1.0 - mix_weight) * anchor_part
        store(4, master_n.at[at], master_o.at[0, at])
    for item in stores + passed:
        item.wait()


def update_call(frag, grad, delta, master, first, second, anchor, momentum, values, igrad, ggrad):
    any_space = pl.BlockSpec(memory_space=pl.ANY)
    like3 = jax.ShapeDtypeStruct((1, R, DV), F32)
    like2 = jax.ShapeDtypeStruct((R, DV), F32)
    dma = pltpu.SemaphoreType.DMA
    whole = pltpu.VMEM((R, DV), F32)
    groups = R // (FRAGS * FR_ROWS)
    return pl.pallas_call(
        update_kernel,
        out_shape=(
            like3, like3, like3, like2, like2,
            jax.ShapeDtypeStruct((1, T, DV), BF16),
            jax.ShapeDtypeStruct((1, T, D), BF16),
            jax.ShapeDtypeStruct((1, D), F32),
        ),
        in_specs=[pl.BlockSpec(memory_space=pltpu.SMEM)]
        + [pl.BlockSpec(memory_space=pltpu.VMEM)] * 7
        + [any_space] * 3,
        out_specs=(any_space,) * 8,
        scratch_shapes=[whole] * 5 + [dma((groups, 5)), dma((3,))],
        compiler_params=pltpu.CompilerParams(vmem_limit_bytes=16 * 1024 * 1024),
        name="update",
    )(frag, grad, delta, master, first, second, anchor, momentum, values, igrad, ggrad)


def body(
    residual, cotangent, norm_gain, master, first_moment, second_moment,
    anchor, outer_momentum, history, fragment, delay,
):
    (
        residual, cotangent, norm_gain, master, first_moment, second_moment,
        anchor, outer_momentum, history, fragment, delay,
    ) = [
        pltpu.with_memory_space_constraint(item, pltpu.HBM)
        for item in (
            residual, cotangent, norm_gain, master, first_moment, second_moment,
            anchor, outer_momentum, history, fragment, delay,
        )
    ]
    values, input_grad, gain_grad, gradient, delta, *carried = main_call(
        fragment, delay, residual, cotangent, norm_gain, master, anchor, history,
        first_moment, second_moment, outer_momentum,
    )
    new_master, new_first, new_second, new_anchor, new_momentum, values, input_grad, gain_grad = update_call(
        fragment, gradient, delta, *carried,
        values, input_grad, gain_grad,
    )
    return (
        values, input_grad, gain_grad, new_master, new_first, new_second, new_anchor, new_momentum,
    )


def solution(mesh):
    rows = P("replica", "fsdp", None)
    both = P("fsdp", None)
    return jax.shard_map(
        body,
        mesh=mesh,
        in_specs=(
            rows, rows, P("replica", None), rows, rows, rows, both, both,
            P("replica", None, "fsdp", None), P(), P("replica", "fsdp"),
        ),
        out_specs=(rows, rows, P("replica", None), rows, rows, rows, both, both),
        check_vma=False,
    )
```
